128 devices in a mesh: seq: 32 (over y_lo, x, z), mp: 4 (over y_hi, core).
Axes of the slice: x: 4, y: 4 (y_hi: 2, y_lo: 2; y = y_hi * 2 + y_lo), z: 4, core: 2. Of those that a mesh axis runs over, the one named last changes fastest.
Arguments:
- tokens: bfloat16 [16384, 5376], P('seq', 'mp'), may hold values from -6 to 6
- q_weight: bfloat16 [5376, 2048], P('seq', 'mp'), may hold values from -0.078125 to 0.078125
- key_matrix: bfloat16 [5376, 1024], P('seq', 'mp'), may hold values from -0.078125 to 0.078125
- value_matrix: bfloat16 [5376, 1024], P('seq', 'mp'), may hold values from -0.078125 to 0.078125
- o_weight: bfloat16 [2048, 5376], P('mp', 'seq'), may hold values from -0.79549513 to 0.79549513
- pre_gain: float32 [5376], replicated, may hold values from 0.1 to 1.9
- post_gain: float32 [5376], P('mp'), may hold values from 0.1 to 1.9
- q_gain: float32 [128], replicated, may hold values from 0.1 to 1.9
- k_gain: float32 [128], replicated, may hold values from 0.1 to 1.9
Outputs:
- layer_out: bfloat16 [16384, 5376], P('seq', 'mp')
The draws below stay inside these ranges and needn't reach their ends.
All inputs are finite; a program needn't handle non-finite values.
Results may differ from the reference program's by a relative error of at most 0.015.
Values may be sent and summed in bfloat16 or wider, within the bound.
No kernel may reach another device: no remote copies, remote signals or barrier semaphores. Data moves between devices by JAX's collectives and lax.ppermute only.
A program may use at most 128 MiB of HBM per device.

```python
import math
import jax
import jax.numpy as jnp
from jax import lax

MODEL_WIDTH = 5376
QUERY_HEADS = 16
KEY_VALUE_HEADS = 8
HEAD_SIZE = 128
WINDOW_LENGTH = 1024
DOCUMENT_TOKENS = 16384
N_MP = 4


def draw_o_weight(key, part):
    key = jax.random.fold_in(key, 5)
    fan_rows = QUERY_HEADS * HEAD_SIZE
    shape = (fan_rows, MODEL_WIDTH)
    column = jnp.arange(MODEL_WIDTH, dtype=jnp.float32) / (MODEL_WIDTH - 1)
    entries = jnp.clip(jax.random.normal(key, shape, jnp.float32), -6.0, 6.0)
    rise = 6.0
    column_scale = rise ** column
    return (entries * column_scale[None, :] * fan_rows ** (-0.5)).astype(jnp.bfloat16)


def steps_of(own_key, extent, pieces, low, largest):
    level = 1.0
    for position, parts in pieces:
        draws = jax.random.uniform(jax.random.fold_in(jax.random.fold_in(own_key, 6), position), (parts,), jnp.float32, low / len(pieces), largest / len(pieces))
        level = level * jnp.repeat(jnp.exp(draws), extent[position] // parts).reshape((-1,) + (1,) * (len(extent) - 1 - position))
    return level


def normal_values(rng, dims, scale, most, shards=(), kind=jnp.bfloat16):
    values = jax.random.normal(rng, dims, jnp.float32) * scale
    if len(shards) > 0:
        values = steps_of(rng, dims, shards, -0.22, 0.18) * values
    return jnp.clip(values, min=-most, max=most).astype(kind)


def setup_inputs(seed: int = 0) -> dict:
    streams_of = jax.random.split(jax.random.key(seed), 10)
    tokens = normal_values(streams_of[0], (DOCUMENT_TOKENS, MODEL_WIDTH), 1.0, 6.0, ((0, 32), (1, 4)))
    q_weight = normal_values(streams_of[1], (MODEL_WIDTH, QUERY_HEADS * HEAD_SIZE), MODEL_WIDTH ** -0.5, 0.078125, ((0, 32), (1, 4)))
    key_matrix = normal_values(streams_of[2], (MODEL_WIDTH, KEY_VALUE_HEADS * HEAD_SIZE), MODEL_WIDTH ** -0.5, 0.078125, ((0, 32), (1, 4)))
    value_matrix = normal_values(streams_of[3], (MODEL_WIDTH, KEY_VALUE_HEADS * HEAD_SIZE), MODEL_WIDTH ** -0.5, 0.078125, ((0, 32), (1, 4)))
    o_weight = draw_o_weight(jax.random.fold_in(streams_of[9], 71), 0)
    pre_gain = jnp.clip(1.0 + 0.18 * jax.random.normal(streams_of[5], (MODEL_WIDTH,), jnp.float32), 0.1, 1.9)
    post_gain = jnp.clip(1.0 + 0.18 * jax.random.normal(streams_of[6], (MODEL_WIDTH,), jnp.float32), 0.1, 1.9)
    q_gain = jnp.clip(1.0 + 0.18 * jax.random.normal(streams_of[7], (HEAD_SIZE,), jnp.float32), 0.1, 1.9)
    k_gain = jnp.clip(1.0 + 0.18 * jax.random.normal(streams_of[8], (HEAD_SIZE,), jnp.float32), 0.1, 1.9)
    return {"tokens": tokens, "q_weight": q_weight, "key_matrix": key_matrix, "value_matrix": value_matrix, "o_weight": o_weight, "pre_gain": pre_gain, "post_gain": post_gain, "q_gain": q_gain, "k_gain": k_gain}


score_scale = 168.0 ** (-0.5)
epsilon = 1e-06

def rms_heads(raw, gain, positions):
    normal = raw * lax.rsqrt(lax.optimization_barrier(jnp.mean(raw * raw, axis=-1, keepdims=True)) + epsilon) * gain
    half = raw.shape[-1] // 2
    freq = 10000.0 ** (-(jnp.arange(half, dtype=jnp.float32) * 2.0) / raw.shape[-1])
    angle = positions.astype(jnp.float32)[:, None] * freq[None, :]
    cosine = jnp.cos(angle)[:, None, :]
    sine = jnp.sin(angle)[:, None, :]
    first = normal[..., :half]
    second = normal[..., half:]
    return jnp.concatenate([first * cosine - second * sine, second * cosine + first * sine], axis=-1)

def reference(tokens, q_weight, key_matrix, value_matrix, o_weight, pre_gain, post_gain, q_gain, k_gain):
    wide = tokens.astype(jnp.float32)
    normed_input = (wide * lax.rsqrt(lax.optimization_barrier(jnp.mean(wide * wide, axis=1, keepdims=True)) + epsilon) * pre_gain).astype(jnp.bfloat16)
    positions = jnp.arange(DOCUMENT_TOKENS, dtype=jnp.int32)
    q_raw = jnp.dot(normed_input, q_weight, preferred_element_type=jnp.float32).reshape(DOCUMENT_TOKENS, QUERY_HEADS, HEAD_SIZE)
    key_unnormed = jnp.dot(normed_input, key_matrix, preferred_element_type=jnp.float32).reshape(DOCUMENT_TOKENS, KEY_VALUE_HEADS, HEAD_SIZE)
    value_vectors = jnp.dot(normed_input, value_matrix, preferred_element_type=jnp.float32).astype(jnp.bfloat16).reshape(DOCUMENT_TOKENS, KEY_VALUE_HEADS, HEAD_SIZE)
    query_vectors = rms_heads(q_raw, q_gain, positions).astype(jnp.bfloat16)
    key_vectors = rms_heads(key_unnormed, k_gain, positions).astype(jnp.bfloat16)
    head_group = QUERY_HEADS // KEY_VALUE_HEADS
    block = math.gcd(DOCUMENT_TOKENS, 512)
    blocks = DOCUMENT_TOKENS // block
    padded_keys = jnp.concatenate([jnp.zeros((WINDOW_LENGTH, KEY_VALUE_HEADS, HEAD_SIZE), jnp.bfloat16), key_vectors], axis=0)
    padded_values = jnp.concatenate([jnp.zeros((WINDOW_LENGTH, KEY_VALUE_HEADS, HEAD_SIZE), jnp.bfloat16), value_vectors], axis=0)
    grouped_queries = query_vectors.reshape(DOCUMENT_TOKENS, KEY_VALUE_HEADS, head_group, HEAD_SIZE)

    def attend(index):
        start = (index * block).astype(jnp.int32)
        query_rows = lax.dynamic_slice_in_dim(grouped_queries, start, block, 0).astype(jnp.float32)
        key_rows = lax.dynamic_slice_in_dim(padded_keys, start, block + WINDOW_LENGTH, 0).astype(jnp.float32)
        value_rows = lax.dynamic_slice_in_dim(padded_values, start, block + WINDOW_LENGTH, 0).astype(jnp.float32)
        scores = jnp.einsum('qkgd,skd->kgqs', query_rows, key_rows) * score_scale
        query_pos = start + jnp.arange(block, dtype=jnp.int32)
        key_pos = start - WINDOW_LENGTH + jnp.arange(block + WINDOW_LENGTH, dtype=jnp.int32)
        distance = query_pos[:, None] - key_pos[None, :]
        allowed = (distance >= 0) & (distance < WINDOW_LENGTH) & (key_pos >= 0)[None, :]
        weights = jnp.where(allowed[None, None], jnp.exp(scores), 0.0)
        denominator = lax.optimization_barrier(jnp.sum(weights, axis=-1))
        probs = weights.astype(jnp.bfloat16).astype(jnp.float32)
        mixed = jnp.einsum('kgqs,skd->qkgd', probs, value_rows)
        mixed = mixed / jnp.transpose(denominator, (2, 0, 1))[..., None]
        return mixed.astype(jnp.bfloat16).reshape(block, QUERY_HEADS * HEAD_SIZE)
    context = lax.map(attend, jnp.arange(blocks, dtype=jnp.int32)).reshape(DOCUMENT_TOKENS, QUERY_HEADS * HEAD_SIZE)
    span = QUERY_HEADS * HEAD_SIZE // N_MP
    attended = jnp.zeros((DOCUMENT_TOKENS, MODEL_WIDTH), jnp.float32)
    for member in range(N_MP):
        part_term = jnp.dot(context[:, member * span:(member + 1) * span], o_weight[member * span:(member + 1) * span], preferred_element_type=jnp.float32)
        attended = attended + part_term.astype(jnp.bfloat16).astype(jnp.float32)
    scale_rows = lax.rsqrt(lax.optimization_barrier(jnp.mean(attended * attended, axis=1, keepdims=True)) + epsilon)
    return (wide + attended * scale_rows * post_gain).astype(jnp.bfloat16)
```

```python
import math

import jax
import jax.numpy as jnp
import numpy as np
from jax import lax
from jax.sharding import Mesh, PartitionSpec as P

MODEL_WIDTH = 5376
HEAD_SIZE = 128
WINDOW_LENGTH = 1024

score_scale = 168.0 ** (-0.5)
epsilon = 1e-06
SEQ = ("yl", "x", "z")
MP = ("yh", "c")


def shift(value, axis, step):
    count = lax.axis_size(axis)
    return lax.ppermute(value, axis, [(i, (i + step) % count) for i in range(count)])


def from_behind(value, steps):
    count = 32
    return lax.ppermute(value, SEQ, [(source, source + steps) for source in range(count - steps)])


def rms_heads(raw, gain, positions):
    normal = raw * lax.rsqrt(jnp.mean(raw * raw, axis=-1, keepdims=True) + epsilon) * gain
    half = raw.shape[-1] // 2
    freq = 10000.0 ** (-(jnp.arange(half, dtype=jnp.float32) * 2.0) / raw.shape[-1])
    angle = positions.astype(jnp.float32)[:, None] * freq[None, :]
    cosine = jnp.cos(angle)[:, None, :]
    sine = jnp.sin(angle)[:, None, :]
    first = normal[..., :half]
    second = normal[..., half:]
    return jnp.concatenate(
        [first * cosine - second * sine, second * cosine + first * sine], axis=-1
    )


def place(buffer, piece, index, axis):
    return lax.dynamic_update_index_in_dim(buffer, piece, index, axis)


def gather_two(own, first, second):
    at = lax.axis_index(first)
    line = jnp.zeros((4,) + own.shape, own.dtype)
    line = place(line, own, at, 0)
    for step in (1, 3, 2):
        line = place(line, shift(own, first, step), (at - step) % 4, 0)
    there = lax.axis_index(second)
    ahead = shift(line, second, 1)
    behind = shift(line, second, 3)
    far_low = shift(ahead[:2], second, 1)
    far_high = shift(behind[2:], second, 3)
    whole = jnp.zeros((4, 4) + own.shape, own.dtype)
    whole = place(whole, line, there, 1)
    whole = place(whole, ahead, (there - 1) % 4, 1)
    whole = place(whole, behind, (there + 1) % 4, 1)
    far = jnp.concatenate([far_low, far_high], axis=0)
    return place(whole, far, (there + 2) % 4, 1)


def local(
    tokens, q_weight, key_matrix, value_matrix, o_weight, pre_gain, post_gain, q_gain, k_gain
):
    rows = tokens.shape[0]
    yl, x, z, yh, c = (lax.axis_index(name) for name in ("yl", "x", "z", "yh", "c"))
    seq_index = (yl * 4 + x) * 4 + z
    whole = lax.all_gather(tokens, MP, axis=1, tiled=True)

    own = jnp.concatenate([q_weight, key_matrix, value_matrix], axis=1)
    other = shift(own, "yl", 1)
    near_weights = gather_two(own, "x", "z")
    far_weights = jnp.swapaxes(gather_two(other, "z", "x"), 0, 1)
    span = 16 * own.shape[0]
    near_weights = near_weights.reshape(span, own.shape[1])
    far_weights = far_weights.reshape(span, own.shape[1])

    turned = o_weight.T
    y = yh * 2 + yl
    flat = lambda p: (p % 2) * 2 + p // 2
    one = lax.ppermute(turned, ("yl", "yh"), [(flat(a), flat(b)) for a, b in ((0, 1), (2, 0), (1, 3), (3, 2))])
    two = lax.ppermute(turned, ("yl", "yh"), [(flat(a), flat(b)) for a, b in ((1, 2), (2, 1))])
    outer = (y == 0) | (y == 3)
    pair = jnp.concatenate([jnp.where(outer, turned, one), jnp.where(outer, one, two)], axis=1)
    out_all = lax.all_gather(pair, ("x", "z"), axis=0, tiled=True)
    half_rows = out_all.shape[0] // 2
    out_mine = lax.dynamic_slice_in_dim(out_all, c * half_rows, half_rows, 0)
    out_theirs = shift(lax.dynamic_slice_in_dim(out_all, (1 - c) * half_rows, half_rows, 0), "c", 1)

    wide = whole.astype(jnp.float32)
    normed = (
        wide * lax.rsqrt(jnp.mean(wide * wide, axis=1, keepdims=True) + epsilon) * pre_gain
    ).astype(jnp.bfloat16)
    near = lax.dynamic_slice_in_dim(normed, yl * span, span, 1)
    far = lax.dynamic_slice_in_dim(normed, (1 - yl) * span, span, 1)
    qkv = jnp.dot(near, near_weights, preferred_element_type=jnp.float32) + jnp.dot(
        far, far_weights, preferred_element_type=jnp.float32
    )
    q_cols = q_weight.shape[1]
    kv_cols = key_matrix.shape[1]
    q_sum = qkv[:, :q_cols]
    k_sum = qkv[:, q_cols : q_cols + kv_cols]
    v_sum = qkv[:, q_cols + kv_cols :]
    base = seq_index * rows
    positions = base + jnp.arange(rows, dtype=jnp.int32)
    local_kv = kv_cols // HEAD_SIZE
    keys_own = rms_heads(k_sum.reshape(rows, local_kv, HEAD_SIZE), k_gain, positions).astype(
        jnp.bfloat16
    )
    values_own = v_sum.astype(jnp.bfloat16)
    stacked = jnp.stack([keys_own.reshape(rows, kv_cols), values_own], axis=0)
    received = [from_behind(stacked, 2), from_behind(stacked, 1)]
    query_vectors = rms_heads(
        q_sum.reshape(rows, q_cols // HEAD_SIZE, HEAD_SIZE), q_gain, positions
    ).astype(jnp.bfloat16)
    joined = jnp.concatenate(received + [stacked], axis=1)
    key_vectors = joined[0].reshape(WINDOW_LENGTH + rows, local_kv, HEAD_SIZE)
    value_vectors = joined[1].reshape(WINDOW_LENGTH + rows, local_kv, HEAD_SIZE)
    head_group = q_cols // HEAD_SIZE // local_kv
    grouped_queries = query_vectors.reshape(rows, local_kv, head_group, HEAD_SIZE)
    scores = (
        jnp.einsum("qkgd,skd->kgqs", grouped_queries, key_vectors, preferred_element_type=jnp.float32)
        * score_scale
    )
    key_pos = base - WINDOW_LENGTH + jnp.arange(rows + WINDOW_LENGTH, dtype=jnp.int32)
    distance = positions[:, None] - key_pos[None, :]
    allowed = (distance >= 0) & (distance < WINDOW_LENGTH) & (key_pos >= 0)[None, :]
    weights = jnp.where(allowed[None, None], jnp.exp(scores), 0.0)
    denominator = jnp.sum(weights, axis=-1)
    mixed = jnp.einsum(
        "kgqs,skd->qkgd",
        weights.astype(jnp.bfloat16),
        value_vectors,
        preferred_element_type=jnp.float32,
    )
    mixed = mixed / jnp.transpose(denominator, (2, 0, 1))[..., None]
    context = mixed.astype(jnp.bfloat16).reshape(rows, q_cols)

    across = shift(context, "yh", 1)
    mine = jnp.concatenate([context, across], axis=1)
    theirs = shift(mine, "c", 1)
    share = lax.dot_general(
        mine, out_mine, (((1,), (1,)), ((), ())), preferred_element_type=jnp.float32
    ) + lax.dot_general(
        theirs, out_theirs, (((1,), (1,)), ((), ())), preferred_element_type=jnp.float32
    )
    total = lax.psum(jnp.sum(share * share, axis=1), MP)
    scale_rows = lax.rsqrt(total / MODEL_WIDTH + epsilon)
    return (tokens.astype(jnp.float32) + share * scale_rows[:, None] * post_gain).astype(
        jnp.bfloat16
    )


def solution(mesh):
    fine = Mesh(np.asarray(mesh.devices).reshape(2, 4, 4, 2, 2), SEQ + MP)
    return jax.shard_map(
        local,
        mesh=fine,
        in_specs=(
            P(SEQ, MP),
            P(SEQ, MP),
            P(SEQ, MP),
            P(SEQ, MP),
            P(MP, SEQ),
            P(),
            P(MP),
            P(),
            P(),
        ),
        out_specs=P(SEQ, MP),
        check_vma=False,
    )
```

```python
import functools

import jax
import jax.numpy as jnp
import numpy as np
from jax import lax
from jax.experimental import pallas as pl
from jax.experimental.pallas import tpu as pltpu
from jax.sharding import Mesh, PartitionSpec as P

MODEL_WIDTH = 5376
HEAD_SIZE = 128
WINDOW_LENGTH = 1024
SHARD = MODEL_WIDTH // 32

score_scale = 168.0 ** (-0.5)
epsilon = 1e-06
SEQ = ("yl", "x", "z")
MP = ("yh", "c")


def shift(value, axis, step):
    count = lax.axis_size(axis)
    return lax.ppermute(value, axis, [(i, (i + step) % count) for i in range(count)])


def from_behind(value, steps):
    count = 32
    return lax.ppermute(value, SEQ, [(source, source + steps) for source in range(count - steps)])


def later(values, done):
    return lax.optimization_barrier((values, done))[0]


def place(buffer, piece, index):
    return lax.dynamic_update_index_in_dim(buffer, piece, index, 0)


def in_line(pieces, at):
    line = jnp.zeros((4,) + pieces[0].shape, pieces[0].dtype)
    for piece, offset in zip(pieces, (0, -1, 1, 2)):
        line = place(line, piece, (at + offset) % 4)
    return line.reshape(4 * pieces[0].shape[0], -1)


def norm_kernel(side, own_ref, other_ref, own_gain, other_gain, near_ref, far_ref):
    own = own_ref[0].astype(jnp.float32)
    other = other_ref[0].astype(jnp.float32)
    total = jnp.sum(own * own, axis=-1, keepdims=True) + jnp.sum(other * other, axis=-1, keepdims=True)
    scale = lax.rsqrt((total[0] + total[1]) / MODEL_WIDTH + epsilon)
    own = (own * scale[None] * own_gain[0]).astype(jnp.bfloat16)
    other = (other * scale[None] * other_gain[0]).astype(jnp.bfloat16)
    for i in range(4):
        for j in range(4):
            start = ((j % 2) * 4 + i) * SHARD
            near_ref[i, :, j * SHARD : (j + 1) * SHARD] = own[j // 2][:, start : start + SHARD]
        far_ref[i] = other[i // 2][:, (i % 2) * 4 * SHARD : ((i % 2) * 4 + 4) * SHARD]


def norm_parts(pieces, gain, side):
    rows = pieces.shape[1]
    width = pieces.shape[2]
    step = 64
    pieces = pieces.reshape(2, 2, rows, width)
    gain = gain.reshape(2, 2, 1, width)
    half = lambda flip: pl.BlockSpec((1, 2, step, width), lambda i, s: (s[flip], 0, i, 0))
    gains = lambda flip: pl.BlockSpec((1, 2, 1, width), lambda i, s: (s[flip], 0, 0, 0))
    out = pl.BlockSpec((4, step, 4 * SHARD), lambda i, s: (0, i, 0))
    shape = jax.ShapeDtypeStruct((4, rows, 4 * SHARD), jnp.bfloat16)
    return pl.pallas_call(
        norm_kernel,
        grid_spec=pltpu.PrefetchScalarGridSpec(
            num_scalar_prefetch=1,
            grid=(rows // step,),
            in_specs=[half(0), half(1), gains(0), gains(1)],
            out_specs=[out, out],
        ),
        out_shape=[shape, shape],
        compiler_params=pltpu.CompilerParams(vmem_limit_bytes=40 << 20),
        cost_estimate=pl.CostEstimate(flops=20_000_000, bytes_accessed=12_000_000, transcendentals=0),
    )(jnp.stack([side, 1 - side]), pieces, pieces, gain, gain)


def accumulate(index, near_ref, far_ref, weights, w_buf, t_buf, sems, total, n_near):
    copies = []
    for k, weight in enumerate(weights):
        source = near_ref if k < n_near else far_ref
        copies.append(
            (
                pltpu.make_async_copy(source.at[index[k]], t_buf.at[k], sems.at[0, k]),
                pltpu.make_async_copy(weight, w_buf.at[k], sems.at[1, k]),
            )
        )
    for pair in copies:
        for copy in pair:
            copy.start()
    rows = total.shape[0]
    for k, pair in enumerate(copies):
        for copy in pair:
            copy.wait()

        @pl.loop(0, rows // 128)
        def _(i):
            at = pl.ds(pl.multiple_of(i * 128, 128), 128)
            part = jnp.dot(t_buf[k, at, :], w_buf[k], preferred_element_type=jnp.float32)
            total[at, :] = part if (k == 0 and n_near == 3) else total[at, :] + part


def early_kernel(index, near_ref, far_ref, *refs):
    weights, (total, w_buf, t_buf, sems) = refs[:6], refs[6:]
    accumulate(index, near_ref, far_ref, weights, w_buf, t_buf, sems, total, 3)


def early_product(index, near, far, weights):
    rows, depth, columns = near.shape[1], near.shape[2], weights[0].shape[1]
    anywhere = pl.BlockSpec(memory_space=pl.ANY)
    count = len(weights)
    return pl.pallas_call(
        early_kernel,
        grid_spec=pltpu.PrefetchScalarGridSpec(
            num_scalar_prefetch=1,
            grid=(1,),
            in_specs=[anywhere] * (2 + count),
            out_specs=pl.BlockSpec((rows, columns), lambda i, s: (0, 0)),
            scratch_shapes=[
                pltpu.VMEM((count, depth, columns), jnp.bfloat16),
                pltpu.VMEM((count, rows, depth), jnp.bfloat16),
                pltpu.SemaphoreType.DMA((2, count)),
            ],
        ),
        out_shape=jax.ShapeDtypeStruct((rows, columns), jnp.float32),
        compiler_params=pltpu.CompilerParams(vmem_limit_bytes=48 << 20),
        cost_estimate=pl.CostEstimate(
            flops=2 * rows * depth * columns * count, bytes_accessed=16_000_000, transcendentals=0
        ),
    )(index, near, far, *weights)


def turned_heads(raw, gain, cosine, sine):
    normal = raw * lax.rsqrt(jnp.mean(raw * raw, axis=-1, keepdims=True) + epsilon) * gain
    return normal * cosine + pltpu.roll(normal, HEAD_SIZE // 2, 1) * sine


def late_kernel(heads, index, near_ref, far_ref, w_near, w_far, before, gain, cosine, sine, out_ref, total, w_buf, t_buf, sems):
    total[...] = before[...]
    accumulate(index, near_ref, far_ref, (w_near, w_far), w_buf, t_buf, sems, total, 1)

    @pl.loop(0, total.shape[0] // 128)
    def _(i):
        at = pl.ds(pl.multiple_of(i * 128, 128), 128)
        for h in range(total.shape[1] // HEAD_SIZE):
            lanes = slice(h * HEAD_SIZE, (h + 1) * HEAD_SIZE)
            raw = total[at, lanes]
            if h < heads:
                raw = turned_heads(raw, gain[...], cosine[at, :], sine[at, :])
            out_ref[at, lanes] = raw.astype(jnp.bfloat16)


def late_product(heads, column, index, near, far, w_near, w_far, before, gain, cosine, sine):
    rows, depth = near.shape[1:]
    columns = w_near.shape[1]
    anywhere = pl.BlockSpec(memory_space=pl.ANY)
    table = pl.BlockSpec((rows, HEAD_SIZE), lambda i, s: (0, 0))
    return pl.pallas_call(
        functools.partial(late_kernel, heads),
        grid_spec=pltpu.PrefetchScalarGridSpec(
            num_scalar_prefetch=1,
            grid=(1,),
            in_specs=[anywhere] * 4
            + [
                pl.BlockSpec((rows, columns), lambda i, s: (0, column)),
                pl.BlockSpec((1, HEAD_SIZE), lambda i, s: (0, 0)),
                table,
                table,
            ],
            out_specs=pl.BlockSpec((rows, columns), lambda i, s: (0, 0)),
            scratch_shapes=[
                pltpu.VMEM((rows, columns), jnp.float32),
                pltpu.VMEM((2, depth, columns), jnp.bfloat16),
                pltpu.VMEM((2, rows, depth), jnp.bfloat16),
                pltpu.SemaphoreType.DMA((2, 2)),
            ],
        ),
        out_shape=jax.ShapeDtypeStruct((rows, columns), jnp.bfloat16),
        compiler_params=pltpu.CompilerParams(vmem_limit_bytes=40 << 20),
        cost_estimate=pl.CostEstimate(
            flops=4 * rows * depth * columns, bytes_accessed=6_000_000, transcendentals=0
        ),
    )(index, near, far, w_near, w_far, before, gain, cosine, sine)


def scores_of(queries, keys):
    score = lax.dot_general(
        queries, keys, (((1,), (1,)), ((), ())), preferred_element_type=jnp.float32
    )
    return jnp.exp(score * score_scale)


def lane_sums(weights):
    parts = [weights[:, i : i + HEAD_SIZE] for i in range(0, weights.shape[1], HEAD_SIZE)]
    return functools.reduce(lambda a, b: a + b, parts)


def both_heads(ref, at):
    return jnp.concatenate([ref[at, :HEAD_SIZE], ref[at, HEAD_SIZE:]], axis=0)


def own_kernel(q_ref, k_ref, v_ref, sum_ref, weight_ref):
    for r in range(q_ref.shape[0] // 128):
        at = slice(r * 128, (r + 1) * 128)
        seen = (r + 1) * 128
        e = scores_of(both_heads(q_ref, at), k_ref[:seen])
        i = lax.broadcasted_iota(jnp.int32, e.shape, 0) % 128
        j = lax.broadcasted_iota(jnp.int32, e.shape, 1)
        e = jnp.where(j <= i + r * 128, e, 0.0)
        mixed = jnp.dot(e.astype(jnp.bfloat16), v_ref[:seen], preferred_element_type=jnp.float32)
        weight = lane_sums(e)
        for h in range(2):
            lanes = slice(h * HEAD_SIZE, (h + 1) * HEAD_SIZE)
            sum_ref[at, lanes] = mixed[h * 128 : (h + 1) * 128]
            weight_ref[at, lanes] = weight[h * 128 : (h + 1) * 128]


def behind_kernel(valid, q_ref, k1_ref, v1_ref, k2_ref, v2_ref, sum_ref, weight_ref, out_ref):
    has_one = valid[0].astype(jnp.float32)
    has_two = valid[1].astype(jnp.float32)
    rows = q_ref.shape[0]
    for r in range(rows // 128):
        at = slice(r * 128, (r + 1) * 128)
        q = both_heads(q_ref, at)
        one = scores_of(q, k1_ref[...])
        two = scores_of(q, k2_ref[r * 128 :])
        i = lax.broadcasted_iota(jnp.int32, two.shape, 0) % 128
        j = lax.broadcasted_iota(jnp.int32, two.shape, 1)
        two = jnp.where(j > i, two, 0.0)
        mixed = has_one * jnp.dot(
            one.astype(jnp.bfloat16), v1_ref[...], preferred_element_type=jnp.float32
        ) + has_two * jnp.dot(
            two.astype(jnp.bfloat16), v2_ref[r * 128 :], preferred_element_type=jnp.float32
        )
        weight = has_one * lane_sums(one) + has_two * lane_sums(two)
        for h in range(2):
            lanes = slice(h * HEAD_SIZE, (h + 1) * HEAD_SIZE)
            top = sum_ref[at, lanes] + mixed[h * 128 : (h + 1) * 128]
            low = jnp.sum(weight_ref[at, lanes] + weight[h * 128 : (h + 1) * 128], axis=-1, keepdims=True)
            out_ref[at, lanes] = (top / low).astype(jnp.bfloat16)


def attend_own(queries, keyed):
    rows, columns = queries.shape
    groups = columns // (2 * HEAD_SIZE)
    pair = pl.BlockSpec((rows, 2 * HEAD_SIZE), lambda g: (0, g))
    shape = jax.ShapeDtypeStruct((rows, columns), jnp.float32)
    return pl.pallas_call(
        own_kernel,
        grid=(groups,),
        in_specs=[
            pair,
            pl.BlockSpec((rows, HEAD_SIZE), lambda g: (0, g)),
            pl.BlockSpec((rows, HEAD_SIZE), lambda g: (0, groups + g)),
        ],
        out_specs=[pair, pair],
        out_shape=[shape, shape],
        compiler_params=pltpu.CompilerParams(vmem_limit_bytes=32 << 20),
        cost_estimate=pl.CostEstimate(
            flops=4 * rows * rows * columns, bytes_accessed=3_000_000, transcendentals=rows * rows * 4
        ),
    )(queries, keyed, keyed)


def attend_behind(valid, queries, one, two, sums, weights):
    rows, columns = queries.shape
    groups = columns // (2 * HEAD_SIZE)
    pair = pl.BlockSpec((rows, 2 * HEAD_SIZE), lambda g, s: (0, g))
    keys = pl.BlockSpec((rows, HEAD_SIZE), lambda g, s: (0, g))
    values = pl.BlockSpec((rows, HEAD_SIZE), lambda g, s: (0, groups + g))
    return pl.pallas_call(
        behind_kernel,
        grid_spec=pltpu.PrefetchScalarGridSpec(
            num_scalar_prefetch=1,
            grid=(groups,),
            in_specs=[pair, keys, values, keys, values, pair, pair],
            out_specs=pair,
        ),
        out_shape=jax.ShapeDtypeStruct((rows, columns), jnp.bfloat16),
        compiler_params=pltpu.CompilerParams(vmem_limit_bytes=32 << 20),
        cost_estimate=pl.CostEstimate(
            flops=8 * rows * rows * columns, bytes_accessed=4_000_000, transcendentals=rows * rows * 8
        ),
    )(valid, queries, one, one, two, two, sums, weights)


def local(
    tokens, q_weight, key_matrix, value_matrix, o_weight, pre_gain, post_gain, q_gain, k_gain
):
    rows = tokens.shape[0]
    q_cols = q_weight.shape[1]
    yl, x, z, yh, c = (lax.axis_index(name) for name in ("yl", "x", "z", "yh", "c"))
    seq_index = (yl * 4 + x) * 4 + z
    whole = lax.all_gather(tokens, MP, axis=0)

    own = jnp.concatenate([q_weight, key_matrix, value_matrix], axis=1)
    other = shift(own, "yl", 1)
    own_line = in_line([own] + [shift(own, "x", step) for step in (1, 3, 2)], x)
    other_line = in_line([other] + [shift(other, "z", step) for step in (1, 3, 2)], z)
    own_line, other_line = lax.optimization_barrier((own_line, other_line))
    own_ahead, own_behind = shift(own_line, "z", 1), shift(own_line, "z", 3)
    other_ahead, other_behind = shift(other_line, "x", 1), shift(other_line, "x", 3)
    own_ahead, own_behind, other_ahead, other_behind = lax.optimization_barrier(
        (own_ahead, own_behind, other_ahead, other_behind)
    )
    own_far_q = shift(own_ahead[:, :q_cols], "z", 1)
    own_far_kv = shift(own_behind[:, q_cols:], "z", 3)
    other_far_q = shift(other_ahead[:, :q_cols], "x", 1)
    other_far_kv = shift(other_behind[:, q_cols:], "x", 3)

    turned = o_weight.T
    y = yh * 2 + yl
    flat = lambda p: (p % 2) * 2 + p // 2
    one = lax.ppermute(turned, ("yl", "yh"), [(flat(a), flat(b)) for a, b in ((0, 1), (2, 0), (1, 3), (3, 2))])
    two = lax.ppermute(turned, ("yl", "yh"), [(flat(a), flat(b)) for a, b in ((1, 2), (2, 1))])
    outer = (y == 0) | (y == 3)
    pair = jnp.concatenate([jnp.where(outer, turned, one), jnp.where(outer, one, two)], axis=1)
    out_all = lax.all_gather(pair, ("x", "z"), axis=0, tiled=True)
    half_rows = out_all.shape[0] // 2
    out_mine = lax.dynamic_slice_in_dim(out_all, c * half_rows, half_rows, 0)
    out_theirs = shift(lax.dynamic_slice_in_dim(out_all, (1 - c) * half_rows, half_rows, 0), "c", 1)

    positions = seq_index * rows + jnp.arange(rows, dtype=jnp.int32)
    half = HEAD_SIZE // 2
    freq = 10000.0 ** (-(jnp.arange(half, dtype=jnp.float32) * 2.0) / HEAD_SIZE)
    angle = positions.astype(jnp.float32)[:, None] * freq[None, :]
    cosine = jnp.cos(angle)
    sine = jnp.sin(angle)
    cosine = jnp.concatenate([cosine, cosine], axis=1)
    sine = jnp.concatenate([-sine, sine], axis=1)

    near, far = norm_parts(whole, pre_gain, yl)
    index = jnp.stack([z, (z + 3) % 4, (z + 1) % 4, x, (x + 3) % 4, (x + 1) % 4])
    total = early_product(
        index, near, far, (own_line, own_ahead, own_behind, other_line, other_ahead, other_behind)
    )
    last = jnp.stack([(z + 2) % 4, (x + 2) % 4])
    keyed = late_product(
        2, 1, last, near, far, own_far_kv, other_far_kv, total, k_gain[None], cosine, sine
    )
    behind_one = from_behind(keyed, 1)
    behind_two = from_behind(keyed, 2)
    queries = late_product(
        4, 0, last, near, far, own_far_q, other_far_q, total, q_gain[None], cosine, sine
    )
    sums, weights = attend_own(queries, keyed)
    valid = jnp.stack([seq_index >= 1, seq_index >= 2]).astype(jnp.int32)
    context = attend_behind(valid, queries, behind_one, behind_two, sums, weights)

    across = shift(context, "yh", 1)
    theirs = shift(context, "c", 1)
    product = lambda a, b: lax.dot_general(
        a, b, (((1,), (1,)), ((), ())), preferred_element_type=jnp.float32
    )
    share = product(context, out_mine[:, :q_cols]) + product(theirs, out_theirs[:, :q_cols])
    theirs_across = shift(across, "c", 1)
    share = share + product(across, out_mine[:, q_cols:]) + product(theirs_across, out_theirs[:, q_cols:])
    total = lax.psum(jnp.sum(share * share, axis=1), MP)
    scale_rows = lax.rsqrt(total / MODEL_WIDTH + epsilon)
    return (tokens.astype(jnp.float32) + share * scale_rows[:, None] * post_gain).astype(
        jnp.bfloat16
    )


def solution(mesh):
    fine = Mesh(np.asarray(mesh.devices).reshape(2, 4, 4, 2, 2), SEQ + MP)
    return jax.shard_map(
        local,
        mesh=fine,
        in_specs=(
            P(SEQ, MP),
            P(SEQ, MP),
            P(SEQ, MP),
            P(SEQ, MP),
            P(MP, SEQ),
            P(),
            P(MP),
            P(),
            P(),
        ),
        out_specs=P(SEQ, MP),
        check_vma=False,
    )
```

```python
import functools

import jax
import jax.numpy as jnp
import numpy as np
from jax import lax
from jax.experimental import pallas as pl
from jax.experimental.pallas import tpu as pltpu
from jax.sharding import Mesh, PartitionSpec as P

MODEL_WIDTH = 5376
HEAD_SIZE = 128
WINDOW_LENGTH = 1024
SHARD = MODEL_WIDTH // 32
VMEM = 56 << 20

score_scale = 168.0 ** (-0.5)
epsilon = 1e-06
SEQ = ("yl", "x", "z")
MP = ("yh", "c")


def shift(value, axis, step):
    count = lax.axis_size(axis)
    return lax.ppermute(value, axis, [(i, (i + step) % count) for i in range(count)])


def from_behind(value, steps):
    count = 32
    return lax.ppermute(value, SEQ, [(source, source + steps) for source in range(count - steps)])


def later(values, done):
    return lax.optimization_barrier((values, done))[0]


def line_kernel(at, *refs):
    pieces, (first, second), sems = refs[:4], refs[4:6], refs[6]
    cut = first.shape[2]
    copies = []
    for k, (piece, offset) in enumerate(zip(pieces, (0, 3, 1, 2))):
        slot = lax.rem(at[0] + offset, 4)
        copies.append(pltpu.make_async_copy(piece.at[:, :cut], first.at[slot], sems.at[0, k]))
        copies.append(pltpu.make_async_copy(piece.at[:, cut:], second.at[slot], sems.at[1, k]))
    for copy in copies:
        copy.start()
    for copy in copies:
        copy.wait()


def in_line(pieces, at, cut):
    depth, columns = pieces[0].shape
    anywhere = pl.BlockSpec(memory_space=pl.ANY)
    shapes = [
        jax.ShapeDtypeStruct((4, depth, cut), jnp.bfloat16),
        jax.ShapeDtypeStruct((4, depth, columns - cut), jnp.bfloat16),
    ]
    first, second = pl.pallas_call(
        line_kernel,
        grid_spec=pltpu.PrefetchScalarGridSpec(
            num_scalar_prefetch=1,
            grid=(1,),
            in_specs=[anywhere] * 4,
            out_specs=[anywhere] * 2,
            scratch_shapes=[pltpu.SemaphoreType.DMA((2, 4))],
        ),
        out_shape=shapes,
        compiler_params=pltpu.CompilerParams(vmem_limit_bytes=VMEM),
        cost_estimate=pl.CostEstimate(flops=0, bytes_accessed=3_000_000, transcendentals=0),
    )(at[None], *pieces)
    return first.reshape(4 * depth, cut), second.reshape(4 * depth, columns - cut)


def norm_kernel(side, own_ref, other_ref, near_gain, far_gain, near_ref, far_ref):
    own = own_ref[0].astype(jnp.float32)
    other = other_ref[0].astype(jnp.float32)
    total = jnp.sum(own * own, axis=(0, 1)) + jnp.sum(other * other, axis=(0, 1))
    scale = lax.rsqrt(total / MODEL_WIDTH + epsilon)[None, None]
    own = own * scale
    other = other * scale
    for i in range(4):
        starts = [(j // 2, ((j % 2) * 4 + i) * SHARD) for j in range(4)]
        part = jnp.concatenate([own[k, s : s + SHARD] for k, s in starts], axis=0)
        near_ref[i] = (part.T * near_gain[0, i]).astype(jnp.bfloat16)
        start = (i % 2) * 4 * SHARD
        part = other[i // 2, start : start + 4 * SHARD]
        far_ref[i] = (part.T * far_gain[0, i]).astype(jnp.bfloat16)


def norm_parts(pieces, gain, side):
    width, rows = pieces.shape[1:]
    step = 128
    pieces = pieces.reshape(2, 2, width, rows)
    far_gain = gain.reshape(2, 4, 4, SHARD)
    near_gain = jnp.swapaxes(far_gain, 1, 2).reshape(2, 4, 1, 4 * SHARD)
    far_gain = far_gain.reshape(2, 4, 1, 4 * SHARD)
    half = lambda flip: pl.BlockSpec((1, 2, width, step), lambda i, s: (s[flip], 0, 0, i))
    gains = lambda flip: pl.BlockSpec((1, 4, 1, 4 * SHARD), lambda i, s: (s[flip], 0, 0, 0))
    out = pl.BlockSpec((4, step, 4 * SHARD), lambda i, s: (0, i, 0))
    shape = jax.ShapeDtypeStruct((4, rows, 4 * SHARD), jnp.bfloat16)
    return pl.pallas_call(
        norm_kernel,
        grid_spec=pltpu.PrefetchScalarGridSpec(
            num_scalar_prefetch=1,
            grid=(rows // step,),
            in_specs=[half(0), half(1), gains(0), gains(1)],
            out_specs=[out, out],
        ),
        out_shape=[shape, shape],
        compiler_params=pltpu.CompilerParams(vmem_limit_bytes=VMEM),
        cost_estimate=pl.CostEstimate(flops=20_000_000, bytes_accessed=12_000_000, transcendentals=0),
    )(jnp.stack([side, 1 - side]), pieces, pieces, near_gain, far_gain)


def accumulate(index, near_ref, far_ref, weights, w_buf, t_buf, sems, total, n_near):
    copies = []
    for k, weight in enumerate(weights):
        source = near_ref if k < n_near else far_ref
        copies.append(
            (
                pltpu.make_async_copy(source.at[index[k]], t_buf.at[k], sems.at[0, k]),
                pltpu.make_async_copy(weight, w_buf.at[k], sems.at[1, k]),
            )
        )
    for pair in copies:
        for copy in pair:
            copy.start()
    for k, pair in enumerate(copies):
        for copy in pair:
            copy.wait()

        @pl.loop(0, total.shape[1] // 256)
        def _(i):
            at = pl.ds(pl.multiple_of(i * 256, 256), 256)
            part = jnp.dot(t_buf[k], w_buf[k, :, at], preferred_element_type=jnp.float32)
            total[:, at] = part if (k == 0 and n_near == 3) else total[:, at] + part


def early_kernel(index, near_ref, far_ref, *refs):
    weights, (total, w_buf, t_buf, sems) = refs[:6], refs[6:]
    accumulate(index, near_ref, far_ref, weights, w_buf, t_buf, sems, total, 3)


def early_product(index, near, far, weights):
    rows, depth, columns = near.shape[1], near.shape[2], weights[0].shape[1]
    anywhere = pl.BlockSpec(memory_space=pl.ANY)
    count = len(weights)
    return pl.pallas_call(
        early_kernel,
        grid_spec=pltpu.PrefetchScalarGridSpec(
            num_scalar_prefetch=1,
            grid=(1,),
            in_specs=[anywhere] * (2 + count),
            out_specs=pl.BlockSpec((rows, columns), lambda i, s: (0, 0)),
            scratch_shapes=[
                pltpu.VMEM((count, depth, columns), jnp.bfloat16),
                pltpu.VMEM((count, rows, depth), jnp.bfloat16),
                pltpu.SemaphoreType.DMA((2, count)),
            ],
        ),
        out_shape=jax.ShapeDtypeStruct((rows, columns), jnp.float32),
        compiler_params=pltpu.CompilerParams(vmem_limit_bytes=VMEM),
        cost_estimate=pl.CostEstimate(
            flops=2 * rows * depth * columns * count, bytes_accessed=10_000_000, transcendentals=0
        ),
    )(index, near, far, *weights)


def turned_heads(raw, gain, cosine, sine):
    normal = raw * lax.rsqrt(jnp.mean(raw * raw, axis=-1, keepdims=True) + epsilon) * gain
    return normal * cosine + pltpu.roll(normal, HEAD_SIZE // 2, 1) * sine


def late_kernel(heads, index, near_ref, far_ref, w_near, w_far, before, gain, cosine, sine, out_ref, total, w_buf, t_buf, sems):
    total[...] = before[...]
    accumulate(index, near_ref, far_ref, (w_near, w_far), w_buf, t_buf, sems, total, 1)

    @pl.loop(0, total.shape[0] // 128)
    def _(i):
        at = pl.ds(pl.multiple_of(i * 128, 128), 128)
        for h in range(total.shape[1] // HEAD_SIZE):
            lanes = slice(h * HEAD_SIZE, (h + 1) * HEAD_SIZE)
            raw = total[at, lanes]
            if h < heads:
                raw = turned_heads(raw, gain[...], cosine[at, :], sine[at, :])
            out_ref[at, lanes] = raw.astype(jnp.bfloat16)


def late_product(heads, index, near, far, w_near, w_far, before, gain, cosine, sine):
    rows, depth = near.shape[1:]
    columns = w_near.shape[1]
    anywhere = pl.BlockSpec(memory_space=pl.ANY)
    table = pl.BlockSpec((rows, HEAD_SIZE), lambda i, s: (0, 0))
    return pl.pallas_call(
        functools.partial(late_kernel, heads),
        grid_spec=pltpu.PrefetchScalarGridSpec(
            num_scalar_prefetch=1,
            grid=(1,),
            in_specs=[anywhere] * 4
            + [
                pl.BlockSpec((rows, columns), lambda i, s: (0, 0)),
                pl.BlockSpec((1, HEAD_SIZE), lambda i, s: (0, 0)),
                table,
                table,
            ],
            out_specs=pl.BlockSpec((rows, columns), lambda i, s: (0, 0)),
            scratch_shapes=[
                pltpu.VMEM((rows, columns), jnp.float32),
                pltpu.VMEM((2, depth, columns), jnp.bfloat16),
                pltpu.VMEM((2, rows, depth), jnp.bfloat16),
                pltpu.SemaphoreType.DMA((2, 2)),
            ],
        ),
        out_shape=jax.ShapeDtypeStruct((rows, columns), jnp.bfloat16),
        compiler_params=pltpu.CompilerParams(vmem_limit_bytes=VMEM),
        cost_estimate=pl.CostEstimate(
            flops=4 * rows * depth * columns, bytes_accessed=6_000_000, transcendentals=0
        ),
    )(index, near, far, w_near, w_far, before, gain, cosine, sine)


def scores_of(queries, keys):
    score = lax.dot_general(
        queries, keys, (((1,), (1,)), ((), ())), preferred_element_type=jnp.float32
    )
    return jnp.exp(score * score_scale)


def lane_sums(weights):
    parts = [weights[:, i : i + HEAD_SIZE] for i in range(0, weights.shape[1], HEAD_SIZE)]
    return functools.reduce(lambda a, b: a + b, parts)


def both_heads(ref, at):
    return jnp.concatenate([ref[at, :HEAD_SIZE], ref[at, HEAD_SIZE:]], axis=0)


def own_kernel(q_ref, k_ref, v_ref, sum_ref, weight_ref):
    for r in range(q_ref.shape[0] // 128):
        at = slice(r * 128, (r + 1) * 128)
        seen = (r + 1) * 128
        e = scores_of(both_heads(q_ref, at), k_ref[:seen])
        i = lax.broadcasted_iota(jnp.int32, e.shape, 0) % 128
        j = lax.broadcasted_iota(jnp.int32, e.shape, 1)
        e = jnp.where(j <= i + r * 128, e, 0.0)
        mixed = jnp.dot(e.astype(jnp.bfloat16), v_ref[:seen], preferred_element_type=jnp.float32)
        weight = lane_sums(e)
        for h in range(2):
            lanes = slice(h * HEAD_SIZE, (h + 1) * HEAD_SIZE)
            sum_ref[at, lanes] = mixed[h * 128 : (h + 1) * 128]
            weight_ref[at, lanes] = weight[h * 128 : (h + 1) * 128]


def behind_kernel(valid, q_ref, k1_ref, v1_ref, k2_ref, v2_ref, sum_ref, weight_ref, out_ref):
    has_one = valid[0].astype(jnp.float32)
    has_two = valid[1].astype(jnp.float32)
    rows = q_ref.shape[0]
    for r in range(rows // 128):
        at = slice(r * 128, (r + 1) * 128)
        q = both_heads(q_ref, at)
        one = scores_of(q, k1_ref[...])
        two = scores_of(q, k2_ref[r * 128 :])
        i = lax.broadcasted_iota(jnp.int32, two.shape, 0) % 128
        j = lax.broadcasted_iota(jnp.int32, two.shape, 1)
        two = jnp.where(j > i, two, 0.0)
        mixed = has_one * jnp.dot(
            one.astype(jnp.bfloat16), v1_ref[...], preferred_element_type=jnp.float32
        ) + has_two * jnp.dot(
            two.astype(jnp.bfloat16), v2_ref[r * 128 :], preferred_element_type=jnp.float32
        )
        weight = has_one * lane_sums(one) + has_two * lane_sums(two)
        for h in range(2):
            lanes = slice(h * HEAD_SIZE, (h + 1) * HEAD_SIZE)
            top = sum_ref[at, lanes] + mixed[h * 128 : (h + 1) * 128]
            low = jnp.sum(weight_ref[at, lanes] + weight[h * 128 : (h + 1) * 128], axis=-1, keepdims=True)
            out_ref[at, lanes] = (top / low).astype(jnp.bfloat16)


def attend_own(queries, keyed):
    rows, columns = queries.shape
    groups = columns // (2 * HEAD_SIZE)
    pair = pl.BlockSpec((rows, 2 * HEAD_SIZE), lambda g: (0, g))
    shape = jax.ShapeDtypeStruct((rows, columns), jnp.float32)
    return pl.pallas_call(
        own_kernel,
        grid=(groups,),
        in_specs=[
            pair,
            pl.BlockSpec((rows, HEAD_SIZE), lambda g: (0, g)),
            pl.BlockSpec((rows, HEAD_SIZE), lambda g: (0, groups + g)),
        ],
        out_specs=[pair, pair],
        out_shape=[shape, shape],
        compiler_params=pltpu.CompilerParams(vmem_limit_bytes=VMEM),
        cost_estimate=pl.CostEstimate(
            flops=4 * rows * rows * columns, bytes_accessed=3_000_000, transcendentals=rows * rows * 4
        ),
    )(queries, keyed, keyed)


def attend_behind(valid, queries, one, two, sums, weights):
    rows, columns = queries.shape
    groups = columns // (2 * HEAD_SIZE)
    pair = pl.BlockSpec((rows, 2 * HEAD_SIZE), lambda g, s: (0, g))
    keys = pl.BlockSpec((rows, HEAD_SIZE), lambda g, s: (0, g))
    values = pl.BlockSpec((rows, HEAD_SIZE), lambda g, s: (0, groups + g))
    return pl.pallas_call(
        behind_kernel,
        grid_spec=pltpu.PrefetchScalarGridSpec(
            num_scalar_prefetch=1,
            grid=(groups,),
            in_specs=[pair, keys, values, keys, values, pair, pair],
            out_specs=pair,
        ),
        out_shape=jax.ShapeDtypeStruct((rows, columns), jnp.bfloat16),
        compiler_params=pltpu.CompilerParams(vmem_limit_bytes=VMEM),
        cost_estimate=pl.CostEstimate(
            flops=8 * rows * rows * columns, bytes_accessed=4_000_000, transcendentals=rows * rows * 8
        ),
    )(valid, queries, one, one, two, two, sums, weights)


def first_kernel(w_ref, c_ref, out_ref):
    out_ref[...] = lax.dot_general(
        w_ref[...], c_ref[...], (((1,), (1,)), ((), ())), preferred_element_type=jnp.float32
    )


def second_kernel(half, w_ref, c_ref, before_ref, out_ref):
    out_ref[...] = (
        before_ref[...]
        + lax.dot_general(
            w_ref[...], c_ref[...], (((1,), (1,)), ((), ())), preferred_element_type=jnp.float32
        )
    ).astype(out_ref.dtype)


def out_first(weight, context):
    rows, depth = context.shape
    columns = weight.shape[0]
    tile = 672
    return pl.pallas_call(
        first_kernel,
        grid=(columns // tile,),
        in_specs=[
            pl.BlockSpec((tile, depth), lambda i: (i, 0)),
            pl.BlockSpec((rows, depth), lambda i: (0, 0)),
        ],
        out_specs=pl.BlockSpec((tile, rows), lambda i: (i, 0)),
        out_shape=jax.ShapeDtypeStruct((columns, rows), jnp.float32),
        compiler_params=pltpu.CompilerParams(vmem_limit_bytes=VMEM),
        cost_estimate=pl.CostEstimate(
            flops=2 * rows * depth * columns, bytes_accessed=9_000_000, transcendentals=0
        ),
    )(weight, context)


def out_second(half, weight, context, before, dtype):
    rows, depth = context.shape
    columns = weight.shape[0] // 2
    tile = 672
    steps = columns // tile
    return pl.pallas_call(
        second_kernel,
        grid_spec=pltpu.PrefetchScalarGridSpec(
            num_scalar_prefetch=1,
            grid=(steps,),
            in_specs=[
                pl.BlockSpec((tile, depth), lambda i, s: (s[0] * steps + i, 1)),
                pl.BlockSpec((rows, depth), lambda i, s: (0, 0)),
                pl.BlockSpec((tile, rows), lambda i, s: (s[0] * steps + i, 0)),
            ],
            out_specs=pl.BlockSpec((tile, rows), lambda i, s: (i, 0)),
        ),
        out_shape=jax.ShapeDtypeStruct((columns, rows), dtype),
        compiler_params=pltpu.CompilerParams(vmem_limit_bytes=VMEM),
        cost_estimate=pl.CostEstimate(
            flops=2 * rows * depth * columns, bytes_accessed=6_000_000, transcendentals=0
        ),
    )(half[None], weight, context, before)


def local(
    tokens, q_weight, key_matrix, value_matrix, o_weight, pre_gain, post_gain, q_gain, k_gain
):
    rows = tokens.shape[0]
    q_cols = q_weight.shape[1]
    yl, x, z, yh, c = (lax.axis_index(name) for name in ("yl", "x", "z", "yh", "c"))
    seq_index = (yl * 4 + x) * 4 + z
    whole = lax.all_gather(tokens.T, MP, axis=0)

    own = jnp.concatenate([q_weight, key_matrix, value_matrix], axis=1)
    other = shift(own, "yl", 1)
    own_pieces = [own] + [shift(own, "x", step) for step in (1, 3, 2)]
    other_pieces = [other] + [shift(other, "z", step) for step in (1, 3, 2)]
    own_q, own_kv = in_line(own_pieces, x, q_cols)
    other_q, other_kv = in_line(other_pieces, z, q_cols)
    own_q, own_kv, other_q, other_kv, turned = lax.optimization_barrier(
        (own_q, own_kv, other_q, other_kv, o_weight.T)
    )
    own_ahead_q, own_behind_kv = shift(own_q, "z", 1), shift(own_kv, "z", 3)
    other_ahead_q, other_behind_kv = shift(other_q, "x", 1), shift(other_kv, "x", 3)
    own_ahead_kv, own_behind_q = shift(own_kv, "z", 1), shift(own_q, "z", 3)
    other_ahead_kv, other_behind_q = shift(other_kv, "x", 1), shift(other_q, "x", 3)
    own_ahead_q, own_behind_kv, other_ahead_q, other_behind_kv, whole = lax.optimization_barrier(
        (own_ahead_q, own_behind_kv, other_ahead_q, other_behind_kv, whole)
    )
    own_far_kv = shift(own_behind_kv, "z", 3)
    other_far_kv = shift(other_behind_kv, "x", 3)
    own_far_q = shift(own_ahead_q, "z", 1)
    other_far_q = shift(other_ahead_q, "x", 1)

    y = yh * 2 + yl
    flat = lambda p: (p % 2) * 2 + p // 2
    one = lax.ppermute(turned, ("yl", "yh"), [(flat(a), flat(b)) for a, b in ((0, 1), (2, 0), (1, 3), (3, 2))])
    two = lax.ppermute(turned, ("yl", "yh"), [(flat(a), flat(b)) for a, b in ((1, 2), (2, 1))])
    outer = (y == 0) | (y == 3)
    pair = jnp.concatenate([jnp.where(outer, turned, one), jnp.where(outer, one, two)], axis=1)
    pair, whole = lax.optimization_barrier((pair, whole))
    out_all = lax.all_gather(pair, ("x", "z"), axis=0, tiled=True)

    positions = seq_index * rows + jnp.arange(rows, dtype=jnp.int32)
    half = HEAD_SIZE // 2
    freq = 10000.0 ** (-(jnp.arange(half, dtype=jnp.float32) * 2.0) / HEAD_SIZE)
    angle = positions.astype(jnp.float32)[:, None] * freq[None, :]
    cosine = jnp.cos(angle)
    sine = jnp.sin(angle)
    cosine = jnp.concatenate([cosine, cosine], axis=1)
    sine = jnp.concatenate([-sine, sine], axis=1)

    near, far = norm_parts(whole, pre_gain, yl)
    index = jnp.stack([z, (z + 3) % 4, (z + 1) % 4, x, (x + 3) % 4, (x + 1) % 4])
    early_kv = early_product(
        index, near, far, (own_kv, own_ahead_kv, own_behind_kv, other_kv, other_ahead_kv, other_behind_kv)
    )
    early_q = early_product(
        index, near, far, (own_q, own_ahead_q, own_behind_q, other_q, other_ahead_q, other_behind_q)
    )
    last = jnp.stack([(z + 2) % 4, (x + 2) % 4])
    keyed = late_product(
        2, last, near, far, own_far_kv, other_far_kv, early_kv, k_gain[None], cosine, sine
    )
    behind_one = from_behind(keyed, 1)
    behind_two = from_behind(keyed, 2)
    queries = late_product(
        4, last, near, far, own_far_q, other_far_q, early_q, q_gain[None], cosine, sine
    )
    sums, weights = attend_own(queries, keyed)
    valid = jnp.stack([seq_index >= 1, seq_index >= 2]).astype(jnp.int32)
    context = attend_behind(valid, queries, behind_one, behind_two, sums, weights)

    across = shift(context, "yh", 1)
    out_all, context = lax.optimization_barrier((out_all, context))
    before = out_first(out_all, context)
    across, before = lax.optimization_barrier((across, before))
    sent = out_second(1 - c, out_all, across, before, jnp.bfloat16)
    received = shift(sent, "c", 1)
    kept = out_second(c, out_all, across, before, jnp.float32)
    share = (kept + received.astype(jnp.float32)).T
    total = lax.psum(jnp.sum(share * share, axis=1), MP)
    scale_rows = lax.rsqrt(total / MODEL_WIDTH + epsilon)
    return (tokens.astype(jnp.float32) + share * scale_rows[:, None] * post_gain).astype(
        jnp.bfloat16
    )


def solution(mesh):
    fine = Mesh(np.asarray(mesh.devices).reshape(2, 4, 4, 2, 2), SEQ + MP)
    return jax.shard_map(
        local,
        mesh=fine,
        in_specs=(
            P(SEQ, MP),
            P(SEQ, MP),
            P(SEQ, MP),
            P(SEQ, MP),
            P(MP, SEQ),
            P(),
            P(MP),
            P(),
            P(),
        ),
        out_specs=P(SEQ, MP),
        check_vma=False,
    )
```

```python
import functools

import jax
import jax.numpy as jnp
import numpy as np
from jax import lax
from jax.experimental import pallas as pl
from jax.experimental.pallas import tpu as pltpu
from jax.sharding import Mesh, PartitionSpec as P

MODEL_WIDTH = 5376
HEAD_SIZE = 128
WINDOW_LENGTH = 1024
SHARD = MODEL_WIDTH // 32
VMEM = 40 << 20
SMALL = 16 << 20

score_scale = 168.0 ** (-0.5)
epsilon = 1e-06
SEQ = ("yl", "x", "z")
MP = ("yh", "c")


def shift(value, axis, step):
    count = lax.axis_size(axis)
    return lax.ppermute(value, axis, [(i, (i + step) % count) for i in range(count)])


def from_behind(value, steps):
    count = 32
    return lax.ppermute(value, SEQ, [(source, source + steps) for source in range(count - steps)])


def later(values, done):
    return lax.optimization_barrier((values, done))[0]


def line_kernel(slots, *refs):
    pieces, (first, second) = refs[:4], refs[4:]
    cut = first.shape[2]
    for k, piece in enumerate(pieces):

        @pl.when(pl.program_id(0) == k)
        def _():
            first[0] = piece[:, :cut]
            second[0] = piece[:, cut:]


def in_line(pieces, at, cut):
    depth, columns = pieces[0].shape
    out = lambda wide: pl.BlockSpec((1, depth, wide), lambda i, s: (s[i], 0, 0))
    first, second = pl.pallas_call(
        line_kernel,
        grid_spec=pltpu.PrefetchScalarGridSpec(
            num_scalar_prefetch=1,
            grid=(4,),
            in_specs=[pl.BlockSpec((depth, columns), lambda i, s: (0, 0))] * 4,
            out_specs=[out(cut), out(columns - cut)],
        ),
        out_shape=[
            jax.ShapeDtypeStruct((4, depth, cut), jnp.bfloat16),
            jax.ShapeDtypeStruct((4, depth, columns - cut), jnp.bfloat16),
        ],
        compiler_params=pltpu.CompilerParams(vmem_limit_bytes=VMEM),
        cost_estimate=pl.CostEstimate(flops=0, bytes_accessed=3_000_000, transcendentals=0),
    )((at + jnp.array([0, 3, 1, 2], jnp.int32)) % 4, *pieces)
    return first.reshape(4 * depth, cut), second.reshape(4 * depth, columns - cut)


def norm_kernel(side, own_ref, other_ref, near_gain, far_gain, near_ref, far_ref):
    own = own_ref[0].astype(jnp.float32)
    other = other_ref[0].astype(jnp.float32)
    total = jnp.sum(own * own, axis=(0, 1)) + jnp.sum(other * other, axis=(0, 1))
    scale = lax.rsqrt(total / MODEL_WIDTH + epsilon)[None, None]
    own = own * scale
    other = other * scale
    for i in range(4):
        starts = [(j // 2, ((j % 2) * 4 + i) * SHARD) for j in range(4)]
        part = jnp.concatenate([own[k, s : s + SHARD] for k, s in starts], axis=0)
        near_ref[i] = (part.T * near_gain[0, i]).astype(jnp.bfloat16)
        start = (i % 2) * 4 * SHARD
        part = other[i // 2, start : start + 4 * SHARD]
        far_ref[i] = (part.T * far_gain[0, i]).astype(jnp.bfloat16)


def norm_parts(pieces, gain, side):
    width, rows = pieces.shape[1:]
    step = 128
    pieces = pieces.reshape(2, 2, width, rows)
    far_gain = gain.reshape(2, 4, 4, SHARD)
    near_gain = jnp.swapaxes(far_gain, 1, 2).reshape(2, 4, 1, 4 * SHARD)
    far_gain = far_gain.reshape(2, 4, 1, 4 * SHARD)
    half = lambda flip: pl.BlockSpec((1, 2, width, step), lambda i, s: (s[flip], 0, 0, i))
    gains = lambda flip: pl.BlockSpec((1, 4, 1, 4 * SHARD), lambda i, s: (s[flip], 0, 0, 0))
    out = pl.BlockSpec((4, step, 4 * SHARD), lambda i, s: (0, i, 0))
    shape = jax.ShapeDtypeStruct((4, rows, 4 * SHARD), jnp.bfloat16)
    return pl.pallas_call(
        norm_kernel,
        grid_spec=pltpu.PrefetchScalarGridSpec(
            num_scalar_prefetch=1,
            grid=(rows // step,),
            in_specs=[half(0), half(1), gains(0), gains(1)],
            out_specs=[out, out],
        ),
        out_shape=[shape, shape],
        compiler_params=pltpu.CompilerParams(vmem_limit_bytes=VMEM),
        cost_estimate=pl.CostEstimate(flops=20_000_000, bytes_accessed=12_000_000, transcendentals=0),
    )(jnp.stack([side, 1 - side]), pieces, pieces, near_gain, far_gain)


def pick(parts, at):
    return lax.dynamic_index_in_dim(parts, at % 4, 0, keepdims=False)


def product(left, right):
    return jnp.dot(left, right, preferred_element_type=jnp.float32)


def turned_heads(raw, gain, cosine, sine):
    normal = raw * lax.rsqrt(jnp.mean(raw * raw, axis=-1, keepdims=True) + epsilon) * gain
    return normal * cosine + pltpu.roll(normal, HEAD_SIZE // 2, 1) * sine


def heads_kernel(heads, raw_ref, gain, cosine, sine, out_ref):
    for h in range(raw_ref.shape[1] // HEAD_SIZE):
        lanes = slice(h * HEAD_SIZE, (h + 1) * HEAD_SIZE)
        raw = raw_ref[:, lanes]
        if h < heads:
            raw = turned_heads(raw, gain[...], cosine[...], sine[...])
        out_ref[:, lanes] = raw.astype(jnp.bfloat16)


def finish_heads(heads, raw, gain, cosine, sine):
    rows, columns = raw.shape
    step = 256
    block = pl.BlockSpec((step, columns), lambda i: (i, 0))
    table = pl.BlockSpec((step, HEAD_SIZE), lambda i: (i, 0))
    return pl.pallas_call(
        functools.partial(heads_kernel, heads),
        grid=(rows // step,),
        in_specs=[block, pl.BlockSpec((1, HEAD_SIZE), lambda i: (0, 0)), table, table],
        out_specs=block,
        out_shape=jax.ShapeDtypeStruct((rows, columns), jnp.bfloat16),
        compiler_params=pltpu.CompilerParams(vmem_limit_bytes=SMALL),
        cost_estimate=pl.CostEstimate(flops=5_000_000, bytes_accessed=3_000_000, transcendentals=0),
    )(raw, gain, cosine, sine)


def scores_of(queries, keys):
    score = lax.dot_general(
        queries, keys, (((1,), (1,)), ((), ())), preferred_element_type=jnp.float32
    )
    return jnp.exp(score * score_scale)


def lane_sums(weights):
    parts = [weights[:, i : i + HEAD_SIZE] for i in range(0, weights.shape[1], HEAD_SIZE)]
    return functools.reduce(lambda a, b: a + b, parts)


def both_heads(ref, at):
    return jnp.concatenate([ref[at, :HEAD_SIZE], ref[at, HEAD_SIZE:]], axis=0)


def own_kernel(q_ref, k_ref, v_ref, sum_ref, weight_ref):
    for r in range(q_ref.shape[0] // 128):
        at = slice(r * 128, (r + 1) * 128)
        seen = (r + 1) * 128
        e = scores_of(both_heads(q_ref, at), k_ref[:seen])
        i = lax.broadcasted_iota(jnp.int32, e.shape, 0) % 128
        j = lax.broadcasted_iota(jnp.int32, e.shape, 1)
        e = jnp.where(j <= i + r * 128, e, 0.0)
        mixed = jnp.dot(e.astype(jnp.bfloat16), v_ref[:seen], preferred_element_type=jnp.float32)
        weight = lane_sums(e)
        for h in range(2):
            lanes = slice(h * HEAD_SIZE, (h + 1) * HEAD_SIZE)
            sum_ref[at, lanes] = mixed[h * 128 : (h + 1) * 128]
            weight_ref[at, lanes] = weight[h * 128 : (h + 1) * 128]


def behind_kernel(valid, q_ref, k1_ref, v1_ref, k2_ref, v2_ref, sum_ref, weight_ref, out_ref):
    has_one = valid[0].astype(jnp.float32)
    has_two = valid[1].astype(jnp.float32)
    rows = q_ref.shape[0]
    for r in range(rows // 128):
        at = slice(r * 128, (r + 1) * 128)
        q = both_heads(q_ref, at)
        one = scores_of(q, k1_ref[...])
        two = scores_of(q, k2_ref[r * 128 :])
        i = lax.broadcasted_iota(jnp.int32, two.shape, 0) % 128
        j = lax.broadcasted_iota(jnp.int32, two.shape, 1)
        two = jnp.where(j > i, two, 0.0)
        mixed = has_one * jnp.dot(
            one.astype(jnp.bfloat16), v1_ref[...], preferred_element_type=jnp.float32
        ) + has_two * jnp.dot(
            two.astype(jnp.bfloat16), v2_ref[r * 128 :], preferred_element_type=jnp.float32
        )
        weight = has_one * lane_sums(one) + has_two * lane_sums(two)
        for h in range(2):
            lanes = slice(h * HEAD_SIZE, (h + 1) * HEAD_SIZE)
            top = sum_ref[at, lanes] + mixed[h * 128 : (h + 1) * 128]
            low = jnp.sum(weight_ref[at, lanes] + weight[h * 128 : (h + 1) * 128], axis=-1, keepdims=True)
            out_ref[at, lanes] = (top / low).astype(jnp.bfloat16)


def attend_own(queries, keyed):
    rows, columns = queries.shape
    groups = columns // (2 * HEAD_SIZE)
    pair = pl.BlockSpec((rows, 2 * HEAD_SIZE), lambda g: (0, g))
    shape = jax.ShapeDtypeStruct((rows, columns), jnp.float32)
    return pl.pallas_call(
        own_kernel,
        grid=(groups,),
        in_specs=[
            pair,
            pl.BlockSpec((rows, HEAD_SIZE), lambda g: (0, g)),
            pl.BlockSpec((rows, HEAD_SIZE), lambda g: (0, groups + g)),
        ],
        out_specs=[pair, pair],
        out_shape=[shape, shape],
        compiler_params=pltpu.CompilerParams(vmem_limit_bytes=SMALL),
        cost_estimate=pl.CostEstimate(
            flops=4 * rows * rows * columns, bytes_accessed=3_000_000, transcendentals=rows * rows * 4
        ),
    )(queries, keyed, keyed)


def attend_behind(valid, queries, one, two, sums, weights):
    rows, columns = queries.shape
    groups = columns // (2 * HEAD_SIZE)
    pair = pl.BlockSpec((rows, 2 * HEAD_SIZE), lambda g, s: (0, g))
    keys = pl.BlockSpec((rows, HEAD_SIZE), lambda g, s: (0, g))
    values = pl.BlockSpec((rows, HEAD_SIZE), lambda g, s: (0, groups + g))
    return pl.pallas_call(
        behind_kernel,
        grid_spec=pltpu.PrefetchScalarGridSpec(
            num_scalar_prefetch=1,
            grid=(groups,),
            in_specs=[pair, keys, values, keys, values, pair, pair],
            out_specs=pair,
        ),
        out_shape=jax.ShapeDtypeStruct((rows, columns), jnp.bfloat16),
        compiler_params=pltpu.CompilerParams(vmem_limit_bytes=SMALL),
        cost_estimate=pl.CostEstimate(
            flops=8 * rows * rows * columns, bytes_accessed=4_000_000, transcendentals=rows * rows * 8
        ),
    )(valid, queries, one, one, two, two, sums, weights)


def gather_out(own, first, second):
    depth, columns = own.shape
    at = lax.axis_index(first)
    line = jnp.zeros((4, depth, columns), own.dtype)
    for step in (0, 1, 3, 2):
        piece = own if step == 0 else shift(own, first, step)
        line = lax.dynamic_update_index_in_dim(line, piece, (at - step) % 4, 0)
    ahead, behind = shift(line, second, 1), shift(line, second, 3)
    low, high = shift(ahead[:2], second, 1), shift(behind[2:], second, 3)
    there = lax.axis_index(second)
    whole = jnp.zeros((4, 4, depth, columns), own.dtype)
    for piece, offset, start in ((line, 0, 0), (ahead, 3, 0), (behind, 1, 0), (low, 2, 0), (high, 2, 2)):
        place = (there + offset) % 4
        if first == "x":
            whole = lax.dynamic_update_slice(whole, piece[:, None], (start, place, 0, 0))
        else:
            whole = lax.dynamic_update_slice(whole, piece[None], (place, start, 0, 0))
    return whole.reshape(16 * depth, columns)


def local(
    tokens, q_weight, key_matrix, value_matrix, o_weight, pre_gain, post_gain, q_gain, k_gain
):
    rows = tokens.shape[0]
    q_cols = q_weight.shape[1]
    yl, x, z, yh, c = (lax.axis_index(name) for name in ("yl", "x", "z", "yh", "c"))
    seq_index = (yl * 4 + x) * 4 + z
    whole = lax.all_gather(tokens.T, MP, axis=0)

    own = jnp.concatenate([q_weight, key_matrix, value_matrix], axis=1)
    other = shift(own, "yl", 1)
    own_pieces = [own] + [shift(own, "x", step) for step in (1, 3, 2)]
    other_pieces = [other] + [shift(other, "z", step) for step in (1, 3, 2)]
    own_q, own_kv = in_line(own_pieces, x, q_cols)
    other_q, other_kv = in_line(other_pieces, z, q_cols)
    own_ahead_q, own_behind_kv = shift(own_q, "z", 1), shift(own_kv, "z", 3)
    other_ahead_q, other_behind_kv = shift(other_q, "x", 1), shift(other_kv, "x", 3)
    own_ahead_kv, own_behind_q = shift(own_kv, "z", 1), shift(own_q, "z", 3)
    other_ahead_kv, other_behind_q = shift(other_kv, "x", 1), shift(other_q, "x", 3)
    own_ahead_q, own_behind_kv, other_ahead_q, other_behind_kv, whole, turned = lax.optimization_barrier(
        (own_ahead_q, own_behind_kv, other_ahead_q, other_behind_kv, whole, o_weight.T)
    )
    own_far_kv = shift(own_behind_kv, "z", 3)
    other_far_kv = shift(other_behind_kv, "x", 3)
    own_far_q = shift(own_ahead_q, "z", 1)
    other_far_q = shift(other_ahead_q, "x", 1)
    near, far = norm_parts(whole, pre_gain, yl)
    part_kv = product(pick(near, z), own_kv) + product(pick(far, x), other_kv)
    part_q = product(pick(near, z), own_q) + product(pick(far, x), other_q)
    part_kv = part_kv + product(pick(near, z + 3), own_ahead_kv) + product(pick(near, z + 1), own_behind_kv)
    part_kv = part_kv + product(pick(far, x + 3), other_ahead_kv) + product(pick(far, x + 1), other_behind_kv)

    y = yh * 2 + yl
    flat = lambda p: (p % 2) * 2 + p // 2
    one = lax.ppermute(turned, ("yl", "yh"), [(flat(a), flat(b)) for a, b in ((0, 1), (2, 0), (1, 3), (3, 2))])
    two = lax.ppermute(turned, ("yl", "yh"), [(flat(a), flat(b)) for a, b in ((1, 2), (2, 1))])
    outer = (y == 0) | (y == 3)
    out_same, out_other = jnp.where(outer, turned, one), jnp.where(outer, one, two)
    out_same, out_other, own_far_kv, other_far_kv = lax.optimization_barrier(
        (out_same, out_other, own_far_kv, other_far_kv)
    )
    out_same = gather_out(out_same, "x", "z")
    out_other = gather_out(out_other, "z", "x")

    positions = seq_index * rows + jnp.arange(rows, dtype=jnp.int32)
    half = HEAD_SIZE // 2
    freq = 10000.0 ** (-(jnp.arange(half, dtype=jnp.float32) * 2.0) / HEAD_SIZE)
    angle = positions.astype(jnp.float32)[:, None] * freq[None, :]
    cosine = jnp.cos(angle)
    sine = jnp.sin(angle)
    cosine = jnp.concatenate([cosine, cosine], axis=1)
    sine = jnp.concatenate([-sine, sine], axis=1)

    part_kv = part_kv + product(pick(near, z + 2), own_far_kv) + product(pick(far, x + 2), other_far_kv)
    keyed = finish_heads(2, part_kv, k_gain[None], cosine, sine)
    behind_one = from_behind(keyed, 1)
    behind_two = from_behind(keyed, 2)
    part_q = part_q + product(pick(near, z + 3), own_ahead_q) + product(pick(near, z + 1), own_behind_q)
    part_q = part_q + product(pick(far, x + 3), other_ahead_q) + product(pick(far, x + 1), other_behind_q)
    part_q = part_q + product(pick(near, z + 2), own_far_q) + product(pick(far, x + 2), other_far_q)
    queries = finish_heads(4, part_q, q_gain[None], cosine, sine)
    sums, weights = attend_own(queries, keyed)
    valid = jnp.stack([seq_index >= 1, seq_index >= 2]).astype(jnp.int32)
    context = attend_behind(valid, queries, behind_one, behind_two, sums, weights)

    across = shift(context, "yh", 1)
    summed = lambda weight, value: lax.dot_general(
        weight, value, (((1,), (1,)), ((), ())), preferred_element_type=jnp.float32
    )
    before = summed(out_same, context)
    across, before = lax.optimization_barrier((across, before))
    columns = out_same.shape[0] // 2

    def half_of(core):
        weight = lax.dynamic_slice_in_dim(out_other, core * columns, columns, 0)
        return lax.dynamic_slice_in_dim(before, core * columns, columns, 0) + summed(weight, across)

    received = shift(half_of(1 - c).astype(jnp.bfloat16), "c", 1)
    share = (half_of(c) + received.astype(jnp.float32)).T
    total = lax.psum(jnp.sum(share * share, axis=1), MP)
    scale_rows = lax.rsqrt(total / MODEL_WIDTH + epsilon)
    return (tokens.astype(jnp.float32) + share * scale_rows[:, None] * post_gain).astype(
        jnp.bfloat16
    )


def solution(mesh):
    fine = Mesh(np.asarray(mesh.devices).reshape(2, 4, 4, 2, 2), SEQ + MP)
    return jax.shard_map(
        local,
        mesh=fine,
        in_specs=(
            P(SEQ, MP),
            P(SEQ, MP),
            P(SEQ, MP),
            P(SEQ, MP),
            P(MP, SEQ),
            P(),
            P(MP),
            P(),
            P(),
        ),
        out_specs=P(SEQ, MP),
        check_vma=False,
    )
```

```python
import functools

import jax
import jax.numpy as jnp
import numpy as np
from jax import lax
from jax.experimental import pallas as pl
from jax.experimental.pallas import tpu as pltpu
from jax.sharding import Mesh, PartitionSpec as P

MODEL_WIDTH = 5376
HEAD_SIZE = 128
WINDOW_LENGTH = 1024
SHARD = MODEL_WIDTH // 32
VMEM = 40 << 20
SMALL = 16 << 20
LARGE = 58 << 20
QUICK = pl.CostEstimate(flops=0, bytes_accessed=0, transcendentals=0)

score_scale = 168.0 ** (-0.5)
epsilon = 1e-06
SEQ = ("yl", "x", "z")
MP = ("yh", "c")


def shift(value, axis, step):
    count = lax.axis_size(axis)
    return lax.ppermute(value, axis, [(i, (i + step) % count) for i in range(count)])


def from_behind(value, steps):
    count = 32
    return lax.ppermute(value, SEQ, [(source, source + steps) for source in range(count - steps)])


def later(values, done):
    return lax.optimization_barrier((values, done))[0]


def line_kernel(slots, *refs):
    for k, piece in enumerate(refs[:4]):

        @pl.when(pl.program_id(0) == k)
        def _():
            refs[4][0] = piece[...]


def in_line(pieces, at):
    depth, columns = pieces[0].shape
    line = pl.pallas_call(
        line_kernel,
        grid_spec=pltpu.PrefetchScalarGridSpec(
            num_scalar_prefetch=1,
            grid=(4,),
            in_specs=[pl.BlockSpec((depth, columns), lambda i, s: (0, 0))] * 4,
            out_specs=pl.BlockSpec((1, depth, columns), lambda i, s: (s[i], 0, 0)),
        ),
        out_shape=jax.ShapeDtypeStruct((4, depth, columns), jnp.bfloat16),
        compiler_params=pltpu.CompilerParams(vmem_limit_bytes=VMEM),
        cost_estimate=QUICK,
    )((at + jnp.array([0, 3, 1, 2], jnp.int32)) % 4, *pieces)
    return line.reshape(4 * depth, columns)


def beside_kernel(*refs):
    out_ref, start = refs[-1], 0
    for ref in refs[:-1]:
        out_ref[:, start : start + ref.shape[1]] = ref[...]
        start += ref.shape[1]


def beside(*values):
    rows, columns = values[0].shape[0], sum(value.shape[1] for value in values)
    return pl.pallas_call(
        beside_kernel,
        out_shape=jax.ShapeDtypeStruct((rows, columns), values[0].dtype),
        compiler_params=pltpu.CompilerParams(vmem_limit_bytes=LARGE),
        cost_estimate=QUICK,
    )(*values)


def cut_kernel(value_ref, out_ref):
    out_ref[...] = value_ref[...]


def cut(value, part):
    rows, columns = value.shape
    step = rows // 2
    return pl.pallas_call(
        cut_kernel,
        grid=(2,),
        in_specs=[pl.BlockSpec((step, columns // 2), lambda i: (i, part))],
        out_specs=pl.BlockSpec((step, columns // 2), lambda i: (i, 0)),
        out_shape=jax.ShapeDtypeStruct((rows, columns // 2), value.dtype),
        compiler_params=pltpu.CompilerParams(vmem_limit_bytes=VMEM),
        cost_estimate=QUICK,
    )(value)


def norm_kernel(side, own_ref, other_ref, near_gain, far_gain, near_ref, far_ref):
    own = own_ref[0].astype(jnp.float32)
    other = other_ref[0].astype(jnp.float32)
    total = jnp.sum(own * own, axis=(0, 1)) + jnp.sum(other * other, axis=(0, 1))
    scale = lax.rsqrt(total / MODEL_WIDTH + epsilon)[None, None]
    own = own * scale
    other = other * scale
    for i in range(4):
        starts = [(j // 2, ((j % 2) * 4 + i) * SHARD) for j in range(4)]
        part = jnp.concatenate([own[k, s : s + SHARD] for k, s in starts], axis=0)
        near_ref[i] = (part.T * near_gain[0, i]).astype(jnp.bfloat16)
        start = (i % 2) * 4 * SHARD
        part = other[i // 2, start : start + 4 * SHARD]
        far_ref[i] = (part.T * far_gain[0, i]).astype(jnp.bfloat16)


def norm_parts(pieces, gain, side):
    width, rows = pieces.shape[1:]
    step = 128
    pieces = pieces.reshape(2, 2, width, rows)
    far_gain = gain.reshape(2, 4, 4, SHARD)
    near_gain = jnp.swapaxes(far_gain, 1, 2).reshape(2, 4, 1, 4 * SHARD)
    far_gain = far_gain.reshape(2, 4, 1, 4 * SHARD)
    half = lambda flip: pl.BlockSpec((1, 2, width, step), lambda i, s: (s[flip], 0, 0, i))
    gains = lambda flip: pl.BlockSpec((1, 4, 1, 4 * SHARD), lambda i, s: (s[flip], 0, 0, 0))
    out = pl.BlockSpec((4, step, 4 * SHARD), lambda i, s: (0, i, 0))
    shape = jax.ShapeDtypeStruct((4, rows, 4 * SHARD), jnp.bfloat16)
    return pl.pallas_call(
        norm_kernel,
        grid_spec=pltpu.PrefetchScalarGridSpec(
            num_scalar_prefetch=1,
            grid=(rows // step,),
            in_specs=[half(0), half(1), gains(0), gains(1)],
            out_specs=[out, out],
        ),
        out_shape=[shape, shape],
        compiler_params=pltpu.CompilerParams(vmem_limit_bytes=LARGE),
        cost_estimate=QUICK,
    )(jnp.stack([side, 1 - side]), pieces, pieces, near_gain, far_gain)


def early_kernel(n_near, count, side, index, near_ref, far_ref, *refs):
    weights, (total, w_buf, t_buf, sems) = refs[:count], refs[count:]
    columns = total.shape[1]
    copies = []
    for k in range(count):
        source = near_ref if k < n_near else far_ref
        weight = weights[k].at[:, side * columns : (side + 1) * columns]
        copies.append(
            (
                pltpu.make_async_copy(source.at[index[k]], t_buf.at[k], sems.at[0, k]),
                pltpu.make_async_copy(weight, w_buf.at[k], sems.at[1, k]),
            )
        )
    for pair in copies:
        for copy in pair:
            copy.start()
    for k, pair in enumerate(copies):
        for copy in pair:
            copy.wait()
        part = jnp.dot(t_buf[k], w_buf[k], preferred_element_type=jnp.float32)
        total[...] = part if k == 0 else total[...] + part


def early_product(side, index, near, far, near_weights, far_weights):
    weights = near_weights + far_weights
    rows, depth, columns = near.shape[1], near.shape[2], weights[0].shape[1] // 2
    anywhere = pl.BlockSpec(memory_space=pl.ANY)
    count = len(weights)
    return pl.pallas_call(
        functools.partial(early_kernel, len(near_weights), count, side),
        grid_spec=pltpu.PrefetchScalarGridSpec(
            num_scalar_prefetch=1,
            grid=(1,),
            in_specs=[anywhere] * (2 + count),
            out_specs=pl.BlockSpec((rows, columns), lambda i, s: (0, 0)),
            scratch_shapes=[
                pltpu.VMEM((count, depth, columns), jnp.bfloat16),
                pltpu.VMEM((count, rows, depth), jnp.bfloat16),
                pltpu.SemaphoreType.DMA((2, count)),
            ],
        ),
        out_shape=jax.ShapeDtypeStruct((rows, columns), jnp.float32),
        compiler_params=pltpu.CompilerParams(vmem_limit_bytes=LARGE),
        cost_estimate=QUICK,
    )(index, near, far, *weights)


def pick(parts, at):
    return lax.dynamic_index_in_dim(parts, at % 4, 0, keepdims=False)


def product(left, right):
    return jnp.dot(left, right, preferred_element_type=jnp.float32)


def turned_heads(raw, gain, cosine, sine):
    normal = raw * lax.rsqrt(jnp.mean(raw * raw, axis=-1, keepdims=True) + epsilon) * gain
    return normal * cosine + pltpu.roll(normal, HEAD_SIZE // 2, 1) * sine


def heads_kernel(heads, raw_ref, gain, cosine, sine, out_ref):
    for h in range(raw_ref.shape[1] // HEAD_SIZE):
        lanes = slice(h * HEAD_SIZE, (h + 1) * HEAD_SIZE)
        raw = raw_ref[:, lanes]
        if h < heads:
            raw = turned_heads(raw, gain[...], cosine[...], sine[...])
        out_ref[:, lanes] = raw.astype(jnp.bfloat16)


def finish_heads(heads, raw, gain, cosine, sine):
    rows, columns = raw.shape
    step = 256
    block = pl.BlockSpec((step, columns), lambda i: (i, 0))
    table = pl.BlockSpec((step, HEAD_SIZE), lambda i: (i, 0))
    return pl.pallas_call(
        functools.partial(heads_kernel, heads),
        grid=(rows // step,),
        in_specs=[block, pl.BlockSpec((1, HEAD_SIZE), lambda i: (0, 0)), table, table],
        out_specs=block,
        out_shape=jax.ShapeDtypeStruct((rows, columns), jnp.bfloat16),
        compiler_params=pltpu.CompilerParams(vmem_limit_bytes=SMALL),
        cost_estimate=QUICK,
    )(raw, gain, cosine, sine)


def scores_of(queries, keys):
    score = lax.dot_general(
        queries, keys, (((1,), (1,)), ((), ())), preferred_element_type=jnp.float32
    )
    return jnp.exp(score * score_scale)


def lane_sums(weights):
    parts = [weights[:, i : i + HEAD_SIZE] for i in range(0, weights.shape[1], HEAD_SIZE)]
    return functools.reduce(lambda a, b: a + b, parts)


def both_heads(ref, at):
    return jnp.concatenate([ref[at, :HEAD_SIZE], ref[at, HEAD_SIZE:]], axis=0)


def own_kernel(q_ref, k_ref, v_ref, sum_ref, weight_ref):
    for r in range(q_ref.shape[0] // 128):
        at = slice(r * 128, (r + 1) * 128)
        seen = (r + 1) * 128
        e = scores_of(both_heads(q_ref, at), k_ref[:seen])
        i = lax.broadcasted_iota(jnp.int32, e.shape, 0) % 128
        j = lax.broadcasted_iota(jnp.int32, e.shape, 1)
        e = jnp.where(j <= i + r * 128, e, 0.0)
        mixed = jnp.dot(e.astype(jnp.bfloat16), v_ref[:seen], preferred_element_type=jnp.float32)
        weight = lane_sums(e)
        for h in range(2):
            lanes = slice(h * HEAD_SIZE, (h + 1) * HEAD_SIZE)
            sum_ref[at, lanes] = mixed[h * 128 : (h + 1) * 128]
            weight_ref[at, lanes] = weight[h * 128 : (h + 1) * 128]


def behind_kernel(valid, q_ref, k1_ref, v1_ref, k2_ref, v2_ref, sum_ref, weight_ref, out_ref):
    has_one = valid[0].astype(jnp.float32)
    has_two = valid[1].astype(jnp.float32)
    rows = q_ref.shape[0]
    for r in range(rows // 128):
        at = slice(r * 128, (r + 1) * 128)
        q = both_heads(q_ref, at)
        one = scores_of(q, k1_ref[...])
        two = scores_of(q, k2_ref[r * 128 :])
        i = lax.broadcasted_iota(jnp.int32, two.shape, 0) % 128
        j = lax.broadcasted_iota(jnp.int32, two.shape, 1)
        two = jnp.where(j > i, two, 0.0)
        mixed = has_one * jnp.dot(
            one.astype(jnp.bfloat16), v1_ref[...], preferred_element_type=jnp.float32
        ) + has_two * jnp.dot(
            two.astype(jnp.bfloat16), v2_ref[r * 128 :], preferred_element_type=jnp.float32
        )
        weight = has_one * lane_sums(one) + has_two * lane_sums(two)
        for h in range(2):
            lanes = slice(h * HEAD_SIZE, (h + 1) * HEAD_SIZE)
            top = sum_ref[at, lanes] + mixed[h * 128 : (h + 1) * 128]
            low = jnp.sum(weight_ref[at, lanes] + weight[h * 128 : (h + 1) * 128], axis=-1, keepdims=True)
            out_ref[at, lanes] = (top / low).astype(jnp.bfloat16)


def attend_own(queries, keyed):
    rows, columns = queries.shape
    groups = columns // (2 * HEAD_SIZE)
    pair = pl.BlockSpec((rows, 2 * HEAD_SIZE), lambda g: (0, g))
    shape = jax.ShapeDtypeStruct((rows, columns), jnp.float32)
    return pl.pallas_call(
        own_kernel,
        grid=(groups,),
        in_specs=[
            pair,
            pl.BlockSpec((rows, HEAD_SIZE), lambda g: (0, g)),
            pl.BlockSpec((rows, HEAD_SIZE), lambda g: (0, groups + g)),
        ],
        out_specs=[pair, pair],
        out_shape=[shape, shape],
        compiler_params=pltpu.CompilerParams(vmem_limit_bytes=SMALL),
        cost_estimate=QUICK,
    )(queries, keyed, keyed)


def attend_behind(valid, queries, one, two, sums, weights):
    rows, columns = queries.shape
    groups = columns // (2 * HEAD_SIZE)
    pair = pl.BlockSpec((rows, 2 * HEAD_SIZE), lambda g, s: (0, g))
    keys = pl.BlockSpec((rows, HEAD_SIZE), lambda g, s: (0, g))
    values = pl.BlockSpec((rows, HEAD_SIZE), lambda g, s: (0, groups + g))
    return pl.pallas_call(
        behind_kernel,
        grid_spec=pltpu.PrefetchScalarGridSpec(
            num_scalar_prefetch=1,
            grid=(groups,),
            in_specs=[pair, keys, values, keys, values, pair, pair],
            out_specs=pair,
        ),
        out_shape=jax.ShapeDtypeStruct((rows, columns), jnp.bfloat16),
        compiler_params=pltpu.CompilerParams(vmem_limit_bytes=SMALL),
        cost_estimate=QUICK,
    )(valid, queries, one, one, two, two, sums, weights)


def local(
    tokens, q_weight, key_matrix, value_matrix, o_weight, pre_gain, post_gain, q_gain, k_gain
):
    rows = tokens.shape[0]
    q_cols = q_weight.shape[1]
    yl, x, z, yh, c = (lax.axis_index(name) for name in ("yl", "x", "z", "yh", "c"))
    seq_index = (yl * 4 + x) * 4 + z
    whole = lax.all_gather(tokens.T, MP, axis=0)

    own = beside(q_weight, key_matrix, value_matrix)
    other = shift(own, "yl", 1)
    own_pieces = [own] + [shift(own, "x", step) for step in (1, 3, 2)]
    other_pieces = [other] + [shift(other, "z", step) for step in (1, 3, 2)]
    own_line = in_line(own_pieces, x)
    other_line = in_line(other_pieces, z)
    own_line, turned = lax.optimization_barrier((own_line, o_weight.T))
    own_ahead, own_behind = shift(own_line, "z", 1), shift(own_line, "z", 3)
    other_ahead, other_behind = shift(other_line, "x", 1), shift(other_line, "x", 3)
    near, far = norm_parts(whole, pre_gain, yl)

    y = yh * 2 + yl
    flat = lambda p: (p % 2) * 2 + p // 2
    one = lax.ppermute(turned, ("yl", "yh"), [(flat(a), flat(b)) for a, b in ((0, 1), (2, 0), (1, 3), (3, 2))])
    two = lax.ppermute(turned, ("yl", "yh"), [(flat(a), flat(b)) for a, b in ((1, 2), (2, 1))])
    positions = seq_index * rows + jnp.arange(rows, dtype=jnp.int32)
    half = HEAD_SIZE // 2
    freq = 10000.0 ** (-(jnp.arange(half, dtype=jnp.float32) * 2.0) / HEAD_SIZE)
    angle = positions.astype(jnp.float32)[:, None] * freq[None, :]
    cosine = jnp.cos(angle)
    sine = jnp.sin(angle)
    cosine = jnp.concatenate([cosine, cosine], axis=1)
    sine = jnp.concatenate([-sine, sine], axis=1)
    index = jnp.stack([z, (z + 3) % 4, (z + 1) % 4, x, (x + 3) % 4, (x + 1) % 4])

    own_ahead, own_behind, other_ahead, other_behind, near, far, one, two, cosine, sine, index = (
        lax.optimization_barrier(
            (own_ahead, own_behind, other_ahead, other_behind, near, far, one, two, cosine, sine, index)
        )
    )

    own_far_kv = shift(cut(own_behind, 1), "z", 3)
    other_far_kv = shift(cut(other_behind, 1), "x", 3)
    own_far_q = shift(cut(own_ahead, 0), "z", 1)
    other_far_q = shift(cut(other_ahead, 0), "x", 1)
    outer = (y == 0) | (y == 3)
    pair = jnp.concatenate([jnp.where(outer, turned, one), jnp.where(outer, one, two)], axis=1)
    out_all = lax.all_gather(pair, ("x", "z"), axis=0, tiled=True)
    parts = [own_line, own_ahead, own_behind], [other_line, other_ahead, other_behind]
    part_kv = early_product(1, index, near, far, *parts)
    part_kv, own_far_kv, other_far_kv = lax.optimization_barrier((part_kv, own_far_kv, other_far_kv))


    part_kv = part_kv + product(pick(near, z + 2), own_far_kv) + product(pick(far, x + 2), other_far_kv)
    keyed = finish_heads(2, part_kv, k_gain[None], cosine, sine)
    behind_one = from_behind(keyed, 1)
    behind_two = from_behind(keyed, 2)
    keyed, index = lax.optimization_barrier((keyed, index))
    part_q = early_product(0, index, near, far, *parts)
    part_q = part_q + product(pick(near, z + 2), own_far_q) + product(pick(far, x + 2), other_far_q)
    queries = finish_heads(4, part_q, q_gain[None], cosine, sine)
    sums, weights = attend_own(queries, keyed)
    valid = jnp.stack([seq_index >= 1, seq_index >= 2]).astype(jnp.int32)
    context = attend_behind(valid, queries, behind_one, behind_two, sums, weights)
    across = shift(context, "yh", 1)
    summed = lambda weight, value: lax.dot_general(
        weight, value, (((1,), (1,)), ((), ())), preferred_element_type=jnp.float32
    )
    out_all, context = lax.optimization_barrier((out_all, context))
    before = summed(out_all[:, :q_cols], context)
    across, before = lax.optimization_barrier((across, before))
    columns = out_all.shape[0] // 2

    def half_of(core):
        weight = lax.dynamic_slice(out_all, (core * columns, q_cols), (columns, q_cols))
        return lax.dynamic_slice_in_dim(before, core * columns, columns, 0) + summed(weight, across)

    received = shift(half_of(1 - c).astype(jnp.bfloat16), "c", 1)
    kept, received = lax.optimization_barrier((half_of(c), received))
    share = (kept + received.astype(jnp.float32)).T
    total = lax.psum(jnp.sum(share * share, axis=1), MP)
    scale_rows = lax.rsqrt(total / MODEL_WIDTH + epsilon)
    return (tokens.astype(jnp.float32) + share * scale_rows[:, None] * post_gain).astype(
        jnp.bfloat16
    )


def solution(mesh):
    fine = Mesh(np.asarray(mesh.devices).reshape(2, 4, 4, 2, 2), SEQ + MP)
    return jax.shard_map(
        local,
        mesh=fine,
        in_specs=(
            P(SEQ, MP),
            P(SEQ, MP),
            P(SEQ, MP),
            P(SEQ, MP),
            P(MP, SEQ),
            P(),
            P(MP),
            P(),
            P(),
        ),
        out_specs=P(SEQ, MP),
        check_vma=False,
    )
```

```python
import functools

import jax
import jax.numpy as jnp
import numpy as np
from jax import lax
from jax.experimental import pallas as pl
from jax.experimental.pallas import tpu as pltpu
from jax.sharding import Mesh, PartitionSpec as P

MODEL_WIDTH = 5376
HEAD_SIZE = 128
WINDOW_LENGTH = 1024
SHARD = MODEL_WIDTH // 32
VMEM = 40 << 20
SMALL = 16 << 20
LARGE = 58 << 20
QUICK = pl.CostEstimate(flops=0, bytes_accessed=0, transcendentals=0)

score_scale = 168.0 ** (-0.5)
epsilon = 1e-06
SEQ = ("yl", "x", "z")
MP = ("yh", "c")


def shift(value, axis, step):
    count = lax.axis_size(axis)
    return lax.ppermute(value, axis, [(i, (i + step) % count) for i in range(count)])


def from_behind(value, steps):
    count = 32
    return lax.ppermute(value, SEQ, [(source, source + steps) for source in range(count - steps)])


def later(values, done):
    return lax.optimization_barrier((values, done))[0]


def line_kernel(slots, *refs):
    for k, piece in enumerate(refs[:4]):

        @pl.when(pl.program_id(0) == k)
        def _():
            refs[4][0] = piece[...]


def in_line(pieces, at):
    depth, columns = pieces[0].shape
    line = pl.pallas_call(
        line_kernel,
        grid_spec=pltpu.PrefetchScalarGridSpec(
            num_scalar_prefetch=1,
            grid=(4,),
            in_specs=[pl.BlockSpec((depth, columns), lambda i, s: (0, 0))] * 4,
            out_specs=pl.BlockSpec((1, depth, columns), lambda i, s: (s[i], 0, 0)),
        ),
        out_shape=jax.ShapeDtypeStruct((4, depth, columns), jnp.bfloat16),
        compiler_params=pltpu.CompilerParams(vmem_limit_bytes=VMEM),
        cost_estimate=QUICK,
    )((at + jnp.array([0, 3, 1, 2], jnp.int32)) % 4, *pieces)
    return line.reshape(4 * depth, columns)


def beside_kernel(*refs):
    out_ref, start = refs[-1], 0
    for ref in refs[:-1]:
        out_ref[:, start : start + ref.shape[1]] = ref[...]
        start += ref.shape[1]


def beside(*values):
    rows, columns = values[0].shape[0], sum(value.shape[1] for value in values)
    return pl.pallas_call(
        beside_kernel,
        out_shape=jax.ShapeDtypeStruct((rows, columns), values[0].dtype),
        compiler_params=pltpu.CompilerParams(vmem_limit_bytes=LARGE),
        cost_estimate=QUICK,
    )(*values)


def cut_kernel(value_ref, out_ref):
    out_ref[...] = value_ref[...]


def cut(value, part):
    rows, columns = value.shape
    step = rows // 2
    return pl.pallas_call(
        cut_kernel,
        grid=(2,),
        in_specs=[pl.BlockSpec((step, columns // 2), lambda i: (i, part))],
        out_specs=pl.BlockSpec((step, columns // 2), lambda i: (i, 0)),
        out_shape=jax.ShapeDtypeStruct((rows, columns // 2), value.dtype),
        compiler_params=pltpu.CompilerParams(vmem_limit_bytes=VMEM),
        cost_estimate=QUICK,
    )(value)


def norm_kernel(side, own_ref, other_ref, near_gain, far_gain, near_ref, far_ref):
    own = own_ref[0].astype(jnp.float32)
    other = other_ref[0].astype(jnp.float32)
    total = jnp.sum(own * own, axis=(0, 1)) + jnp.sum(other * other, axis=(0, 1))
    scale = lax.rsqrt(total / MODEL_WIDTH + epsilon)[None, None]
    own = own * scale
    other = other * scale
    for i in range(4):
        starts = [(j // 2, ((j % 2) * 4 + i) * SHARD) for j in range(4)]
        part = jnp.concatenate([own[k, s : s + SHARD] for k, s in starts], axis=0)
        near_ref[i] = (part.T * near_gain[0, i]).astype(jnp.bfloat16)
        start = (i % 2) * 4 * SHARD
        part = other[i // 2, start : start + 4 * SHARD]
        far_ref[i] = (part.T * far_gain[0, i]).astype(jnp.bfloat16)


def norm_parts(pieces, gain, side):
    width, rows = pieces.shape[1:]
    step = 256
    pieces = pieces.reshape(2, 2, width, rows)
    far_gain = gain.reshape(2, 4, 4, SHARD)
    near_gain = jnp.swapaxes(far_gain, 1, 2).reshape(2, 4, 1, 4 * SHARD)
    far_gain = far_gain.reshape(2, 4, 1, 4 * SHARD)
    half = lambda flip: pl.BlockSpec((1, 2, width, step), lambda i, s: (s[flip], 0, 0, i))
    gains = lambda flip: pl.BlockSpec((1, 4, 1, 4 * SHARD), lambda i, s: (s[flip], 0, 0, 0))
    out = pl.BlockSpec((4, step, 4 * SHARD), lambda i, s: (0, i, 0))
    shape = jax.ShapeDtypeStruct((4, rows, 4 * SHARD), jnp.bfloat16)
    return pl.pallas_call(
        norm_kernel,
        grid_spec=pltpu.PrefetchScalarGridSpec(
            num_scalar_prefetch=1,
            grid=(rows // step,),
            in_specs=[half(0), half(1), gains(0), gains(1)],
            out_specs=[out, out],
        ),
        out_shape=[shape, shape],
        compiler_params=pltpu.CompilerParams(vmem_limit_bytes=LARGE),
        cost_estimate=QUICK,
    )(jnp.stack([side, 1 - side]), pieces, pieces, near_gain, far_gain)


def early_kernel(n_near, count, side, index, near_ref, far_ref, *refs):
    weights, (total, w_buf, t_buf, sems) = refs[:count], refs[count:]
    columns = total.shape[1]
    copies = []
    for k in range(count):
        source = near_ref if k < n_near else far_ref
        weight = weights[k].at[:, side * columns : (side + 1) * columns]
        copies.append(
            (
                pltpu.make_async_copy(source.at[index[k]], t_buf.at[k], sems.at[0, k]),
                pltpu.make_async_copy(weight, w_buf.at[k], sems.at[1, k]),
            )
        )
    for pair in copies:
        for copy in pair:
            copy.start()
    for k, pair in enumerate(copies):
        for copy in pair:
            copy.wait()
        part = jnp.dot(t_buf[k], w_buf[k], preferred_element_type=jnp.float32)
        total[...] = part if k == 0 else total[...] + part


def early_product(side, index, near, far, near_weights, far_weights):
    weights = near_weights + far_weights
    rows, depth, columns = near.shape[1], near.shape[2], weights[0].shape[1] // 2
    anywhere = pl.BlockSpec(memory_space=pl.ANY)
    count = len(weights)
    return pl.pallas_call(
        functools.partial(early_kernel, len(near_weights), count, side),
        grid_spec=pltpu.PrefetchScalarGridSpec(
            num_scalar_prefetch=1,
            grid=(1,),
            in_specs=[anywhere] * (2 + count),
            out_specs=pl.BlockSpec((rows, columns), lambda i, s: (0, 0)),
            scratch_shapes=[
                pltpu.VMEM((count, depth, columns), jnp.bfloat16),
                pltpu.VMEM((count, rows, depth), jnp.bfloat16),
                pltpu.SemaphoreType.DMA((2, count)),
            ],
        ),
        out_shape=jax.ShapeDtypeStruct((rows, columns), jnp.float32),
        compiler_params=pltpu.CompilerParams(vmem_limit_bytes=LARGE),
        cost_estimate=QUICK,
    )(index, near, far, *weights)


def pick(parts, at):
    return lax.dynamic_index_in_dim(parts, at % 4, 0, keepdims=False)


def product(left, right):
    return jnp.dot(left, right, preferred_element_type=jnp.float32)


def turned_heads(raw, gain, cosine, sine):
    normal = raw * lax.rsqrt(jnp.mean(raw * raw, axis=-1, keepdims=True) + epsilon) * gain
    return normal * cosine + pltpu.roll(normal, HEAD_SIZE // 2, 1) * sine


def heads_kernel(heads, raw_ref, gain, cosine, sine, out_ref):
    for h in range(raw_ref.shape[1] // HEAD_SIZE):
        lanes = slice(h * HEAD_SIZE, (h + 1) * HEAD_SIZE)
        raw = raw_ref[:, lanes]
        if h < heads:
            raw = turned_heads(raw, gain[...], cosine[...], sine[...])
        out_ref[:, lanes] = raw.astype(jnp.bfloat16)


def finish_heads(heads, raw, gain, cosine, sine):
    rows, columns = raw.shape
    step = 256
    block = pl.BlockSpec((step, columns), lambda i: (i, 0))
    table = pl.BlockSpec((step, HEAD_SIZE), lambda i: (i, 0))
    return pl.pallas_call(
        functools.partial(heads_kernel, heads),
        grid=(rows // step,),
        in_specs=[block, pl.BlockSpec((1, HEAD_SIZE), lambda i: (0, 0)), table, table],
        out_specs=block,
        out_shape=jax.ShapeDtypeStruct((rows, columns), jnp.bfloat16),
        compiler_params=pltpu.CompilerParams(vmem_limit_bytes=SMALL),
        cost_estimate=QUICK,
    )(raw, gain, cosine, sine)


def scores_of(queries, keys):
    score = lax.dot_general(
        queries, keys, (((1,), (1,)), ((), ())), preferred_element_type=jnp.float32
    )
    return jnp.exp(score * score_scale)


def lane_sums(weights):
    parts = [weights[:, i : i + HEAD_SIZE] for i in range(0, weights.shape[1], HEAD_SIZE)]
    return functools.reduce(lambda a, b: a + b, parts)


def both_heads(ref, at):
    return jnp.concatenate([ref[at, :HEAD_SIZE], ref[at, HEAD_SIZE:]], axis=0)


def own_kernel(q_ref, k_ref, v_ref, sum_ref, weight_ref):
    for r in range(q_ref.shape[0] // 128):
        at = slice(r * 128, (r + 1) * 128)
        seen = (r + 1) * 128
        e = scores_of(both_heads(q_ref, at), k_ref[:seen])
        i = lax.broadcasted_iota(jnp.int32, e.shape, 0) % 128
        j = lax.broadcasted_iota(jnp.int32, e.shape, 1)
        e = jnp.where(j <= i + r * 128, e, 0.0)
        mixed = jnp.dot(e.astype(jnp.bfloat16), v_ref[:seen], preferred_element_type=jnp.float32)
        weight = lane_sums(e)
        for h in range(2):
            lanes = slice(h * HEAD_SIZE, (h + 1) * HEAD_SIZE)
            sum_ref[at, lanes] = mixed[h * 128 : (h + 1) * 128]
            weight_ref[at, lanes] = weight[h * 128 : (h + 1) * 128]


def behind_kernel(valid, q_ref, k1_ref, v1_ref, k2_ref, v2_ref, sum_ref, weight_ref, out_ref):
    has_one = valid[0].astype(jnp.float32)
    has_two = valid[1].astype(jnp.float32)
    rows = q_ref.shape[0]
    for r in range(rows // 128):
        at = slice(r * 128, (r + 1) * 128)
        q = both_heads(q_ref, at)
        one = scores_of(q, k1_ref[...])
        two = scores_of(q, k2_ref[r * 128 :])
        i = lax.broadcasted_iota(jnp.int32, two.shape, 0) % 128
        j = lax.broadcasted_iota(jnp.int32, two.shape, 1)
        two = jnp.where(j > i, two, 0.0)
        mixed = has_one * jnp.dot(
            one.astype(jnp.bfloat16), v1_ref[...], preferred_element_type=jnp.float32
        ) + has_two * jnp.dot(
            two.astype(jnp.bfloat16), v2_ref[r * 128 :], preferred_element_type=jnp.float32
        )
        weight = has_one * lane_sums(one) + has_two * lane_sums(two)
        for h in range(2):
            lanes = slice(h * HEAD_SIZE, (h + 1) * HEAD_SIZE)
            top = sum_ref[at, lanes] + mixed[h * 128 : (h + 1) * 128]
            low = jnp.sum(weight_ref[at, lanes] + weight[h * 128 : (h + 1) * 128], axis=-1, keepdims=True)
            out_ref[at, lanes] = (top / low).astype(jnp.bfloat16)


def attend_own(queries, keyed):
    rows, columns = queries.shape
    groups = columns // (2 * HEAD_SIZE)
    pair = pl.BlockSpec((rows, 2 * HEAD_SIZE), lambda g: (0, g))
    shape = jax.ShapeDtypeStruct((rows, columns), jnp.float32)
    return pl.pallas_call(
        own_kernel,
        grid=(groups,),
        in_specs=[
            pair,
            pl.BlockSpec((rows, HEAD_SIZE), lambda g: (0, g)),
            pl.BlockSpec((rows, HEAD_SIZE), lambda g: (0, groups + g)),
        ],
        out_specs=[pair, pair],
        out_shape=[shape, shape],
        compiler_params=pltpu.CompilerParams(vmem_limit_bytes=SMALL),
        cost_estimate=QUICK,
    )(queries, keyed, keyed)


def attend_behind(valid, queries, one, two, sums, weights):
    rows, columns = queries.shape
    groups = columns // (2 * HEAD_SIZE)
    pair = pl.BlockSpec((rows, 2 * HEAD_SIZE), lambda g, s: (0, g))
    keys = pl.BlockSpec((rows, HEAD_SIZE), lambda g, s: (0, g))
    values = pl.BlockSpec((rows, HEAD_SIZE), lambda g, s: (0, groups + g))
    return pl.pallas_call(
        behind_kernel,
        grid_spec=pltpu.PrefetchScalarGridSpec(
            num_scalar_prefetch=1,
            grid=(groups,),
            in_specs=[pair, keys, values, keys, values, pair, pair],
            out_specs=pair,
        ),
        out_shape=jax.ShapeDtypeStruct((rows, columns), jnp.bfloat16),
        compiler_params=pltpu.CompilerParams(vmem_limit_bytes=SMALL),
        cost_estimate=QUICK,
    )(valid, queries, one, one, two, two, sums, weights)


def local(
    tokens, q_weight, key_matrix, value_matrix, o_weight, pre_gain, post_gain, q_gain, k_gain
):
    rows = tokens.shape[0]
    q_cols = q_weight.shape[1]
    yl, x, z, yh, c = (lax.axis_index(name) for name in ("yl", "x", "z", "yh", "c"))
    seq_index = (yl * 4 + x) * 4 + z
    whole = lax.all_gather(tokens.T, MP, axis=0)

    own = beside(q_weight, key_matrix, value_matrix)
    other = shift(own, "yl", 1)
    own_pieces = [own] + [shift(own, "x", step) for step in (1, 3, 2)]
    other_pieces = [other] + [shift(other, "z", step) for step in (1, 3, 2)]
    own_line = in_line(own_pieces, x)
    other_line = in_line(other_pieces, z)
    own_line, turned = lax.optimization_barrier((own_line, o_weight.T))
    own_ahead, own_behind = shift(own_line, "z", 1), shift(own_line, "z", 3)
    other_ahead, other_behind = shift(other_line, "x", 1), shift(other_line, "x", 3)
    near, far = norm_parts(whole, pre_gain, yl)

    y = yh * 2 + yl
    flat = lambda p: (p % 2) * 2 + p // 2
    one = lax.ppermute(turned, ("yl", "yh"), [(flat(a), flat(b)) for a, b in ((0, 1), (2, 0), (1, 3), (3, 2))])
    two = lax.ppermute(turned, ("yl", "yh"), [(flat(a), flat(b)) for a, b in ((1, 2), (2, 1))])
    positions = seq_index * rows + jnp.arange(rows, dtype=jnp.int32)
    half = HEAD_SIZE // 2
    freq = 10000.0 ** (-(jnp.arange(half, dtype=jnp.float32) * 2.0) / HEAD_SIZE)
    angle = positions.astype(jnp.float32)[:, None] * freq[None, :]
    cosine = jnp.cos(angle)
    sine = jnp.sin(angle)
    cosine = jnp.concatenate([cosine, cosine], axis=1)
    sine = jnp.concatenate([-sine, sine], axis=1)
    index = jnp.stack([z, (z + 3) % 4, (z + 1) % 4, x, (x + 3) % 4, (x + 1) % 4])

    own_ahead, own_behind, other_ahead, other_behind, near, far, one, two, cosine, sine, index = (
        lax.optimization_barrier(
            (own_ahead, own_behind, other_ahead, other_behind, near, far, one, two, cosine, sine, index)
        )
    )

    own_far_kv = shift(cut(own_behind, 1), "z", 3)
    other_far_kv = shift(cut(other_behind, 1), "x", 3)
    own_far_q = shift(cut(own_ahead, 0), "z", 1)
    other_far_q = shift(cut(other_ahead, 0), "x", 1)
    outer = (y == 0) | (y == 3)
    pair = jnp.concatenate([jnp.where(outer, turned, one), jnp.where(outer, one, two)], axis=1)
    out_all = lax.all_gather(pair, ("x", "z"), axis=0, tiled=True)
    parts = [own_line, own_ahead, own_behind], [other_line, other_ahead, other_behind]
    part_kv = early_product(1, index, near, far, *parts)
    part_kv, own_far_kv, other_far_kv = lax.optimization_barrier((part_kv, own_far_kv, other_far_kv))


    part_kv = part_kv + product(pick(near, z + 2), own_far_kv) + product(pick(far, x + 2), other_far_kv)
    keyed = finish_heads(2, part_kv, k_gain[None], cosine, sine)
    behind_one = from_behind(keyed, 1)
    behind_two = from_behind(keyed, 2)
    keyed, index = lax.optimization_barrier((keyed, index))
    part_q = early_product(0, index, near, far, *parts)
    part_q = part_q + product(pick(near, z + 2), own_far_q) + product(pick(far, x + 2), other_far_q)
    queries = finish_heads(4, part_q, q_gain[None], cosine, sine)
    sums, weights = attend_own(queries, keyed)
    valid = jnp.stack([seq_index >= 1, seq_index >= 2]).astype(jnp.int32)
    context = attend_behind(valid, queries, behind_one, behind_two, sums, weights)
    across = shift(context, "yh", 1)
    summed = lambda weight, value: lax.dot_general(
        weight, value, (((1,), (1,)), ((), ())), preferred_element_type=jnp.float32
    )
    out_all, context = lax.optimization_barrier((out_all, context))
    both = jnp.concatenate([context, across], axis=1)
    columns = out_all.shape[0] // 2

    def half_of(core):
        return summed(lax.dynamic_slice_in_dim(out_all, core * columns, columns, 0), both)

    received = shift(half_of(1 - c).astype(jnp.bfloat16), "c", 1)
    kept, received = lax.optimization_barrier((half_of(c), received))
    share = (kept + received.astype(jnp.float32)).T
    total = lax.psum(jnp.sum(share * share, axis=1), MP)
    scale_rows = lax.rsqrt(total / MODEL_WIDTH + epsilon)
    return (tokens.astype(jnp.float32) + share * scale_rows[:, None] * post_gain).astype(
        jnp.bfloat16
    )


def solution(mesh):
    fine = Mesh(np.asarray(mesh.devices).reshape(2, 4, 4, 2, 2), SEQ + MP)
    return jax.shard_map(
        local,
        mesh=fine,
        in_specs=(
            P(SEQ, MP),
            P(SEQ, MP),
            P(SEQ, MP),
            P(SEQ, MP),
            P(MP, SEQ),
            P(),
            P(MP),
            P(),
            P(),
        ),
        out_specs=P(SEQ, MP),
        check_vma=False,
    )
```

```python
import functools

import jax
import jax.numpy as jnp
import numpy as np
from jax import lax
from jax.experimental import pallas as pl
from jax.experimental.pallas import tpu as pltpu
from jax.sharding import Mesh, PartitionSpec as P

MODEL_WIDTH = 5376
HEAD_SIZE = 128
WINDOW_LENGTH = 1024
SHARD = MODEL_WIDTH // 32
VMEM = 40 << 20
SMALL = 16 << 20
LARGE = 58 << 20
QUICK = pl.CostEstimate(flops=0, bytes_accessed=0, transcendentals=0)

score_scale = 168.0 ** (-0.5)
epsilon = 1e-06
SEQ = ("yl", "x", "z")
MP = ("yh", "c")


def shift(value, axis, step):
    count = lax.axis_size(axis)
    return lax.ppermute(value, axis, [(i, (i + step) % count) for i in range(count)])


def from_behind(value, steps):
    count = 32
    return lax.ppermute(value, SEQ, [(source, source + steps) for source in range(count - steps)])


def later(values, done):
    return lax.optimization_barrier((values, done))[0]


def line_kernel(slots, *refs):
    for k, piece in enumerate(refs[:4]):

        @pl.when(pl.program_id(0) == k)
        def _():
            refs[4][0] = piece[...]


def in_line(pieces, at):
    depth, columns = pieces[0].shape
    line = pl.pallas_call(
        line_kernel,
        grid_spec=pltpu.PrefetchScalarGridSpec(
            num_scalar_prefetch=1,
            grid=(4,),
            in_specs=[pl.BlockSpec((depth, columns), lambda i, s: (0, 0))] * 4,
            out_specs=pl.BlockSpec((1, depth, columns), lambda i, s: (s[i], 0, 0)),
        ),
        out_shape=jax.ShapeDtypeStruct((4, depth, columns), jnp.bfloat16),
        compiler_params=pltpu.CompilerParams(vmem_limit_bytes=VMEM),
        cost_estimate=QUICK,
    )((at + jnp.array([0, 3, 1, 2], jnp.int32)) % 4, *pieces)
    return line.reshape(4 * depth, columns)


def beside_kernel(*refs):
    out_ref, start = refs[-1], 0
    for ref in refs[:-1]:
        out_ref[:, start : start + ref.shape[1]] = ref[...]
        start += ref.shape[1]


def beside(*values):
    rows, columns = values[0].shape[0], sum(value.shape[1] for value in values)
    return pl.pallas_call(
        beside_kernel,
        out_shape=jax.ShapeDtypeStruct((rows, columns), values[0].dtype),
        compiler_params=pltpu.CompilerParams(vmem_limit_bytes=LARGE),
        cost_estimate=QUICK,
    )(*values)


def cut_kernel(value_ref, out_ref):
    out_ref[...] = value_ref[...]


def cut(value, part):
    rows, columns = value.shape
    step = rows // 2
    return pl.pallas_call(
        cut_kernel,
        grid=(2,),
        in_specs=[pl.BlockSpec((step, columns // 2), lambda i: (i, part))],
        out_specs=pl.BlockSpec((step, columns // 2), lambda i: (i, 0)),
        out_shape=jax.ShapeDtypeStruct((rows, columns // 2), value.dtype),
        compiler_params=pltpu.CompilerParams(vmem_limit_bytes=VMEM),
        cost_estimate=QUICK,
    )(value)


def norm_kernel(side, own_ref, other_ref, near_gain, far_gain, near_ref, far_ref):
    own = own_ref[0].astype(jnp.float32)
    other = other_ref[0].astype(jnp.float32)
    total = jnp.sum(own * own, axis=(0, 1)) + jnp.sum(other * other, axis=(0, 1))
    scale = lax.rsqrt(total / MODEL_WIDTH + epsilon)[None, None]
    own = own * scale
    other = other * scale
    for i in range(4):
        starts = [(j // 2, ((j % 2) * 4 + i) * SHARD) for j in range(4)]
        part = jnp.concatenate([own[k, s : s + SHARD] for k, s in starts], axis=0)
        near_ref[i] = (part.T * near_gain[0, i]).astype(jnp.bfloat16)
        start = (i % 2) * 4 * SHARD
        part = other[i // 2, start : start + 4 * SHARD]
        far_ref[i] = (part.T * far_gain[0, i]).astype(jnp.bfloat16)


def norm_parts(pieces, gain, side):
    width, rows = pieces.shape[1:]
    step = 256
    pieces = pieces.reshape(2, 2, width, rows)
    far_gain = gain.reshape(2, 4, 4, SHARD)
    near_gain = jnp.swapaxes(far_gain, 1, 2).reshape(2, 4, 1, 4 * SHARD)
    far_gain = far_gain.reshape(2, 4, 1, 4 * SHARD)
    half = lambda flip: pl.BlockSpec((1, 2, width, step), lambda i, s: (s[flip], 0, 0, i))
    gains = lambda flip: pl.BlockSpec((1, 4, 1, 4 * SHARD), lambda i, s: (s[flip], 0, 0, 0))
    out = pl.BlockSpec((4, step, 4 * SHARD), lambda i, s: (0, i, 0))
    shape = jax.ShapeDtypeStruct((4, rows, 4 * SHARD), jnp.bfloat16)
    return pl.pallas_call(
        norm_kernel,
        grid_spec=pltpu.PrefetchScalarGridSpec(
            num_scalar_prefetch=1,
            grid=(rows // step,),
            in_specs=[half(0), half(1), gains(0), gains(1)],
            out_specs=[out, out],
        ),
        out_shape=[shape, shape],
        compiler_params=pltpu.CompilerParams(vmem_limit_bytes=LARGE),
        cost_estimate=QUICK,
    )(jnp.stack([side, 1 - side]), pieces, pieces, near_gain, far_gain)


def early_kernel(n_near, count, side, index, near_ref, far_ref, *refs):
    weights, (total, w_buf, t_buf, sems) = refs[:count], refs[count:]
    columns = total.shape[1]
    copies = []
    for k in range(count):
        source = near_ref if k < n_near else far_ref
        weight = weights[k].at[:, side * columns : (side + 1) * columns]
        copies.append(
            (
                pltpu.make_async_copy(source.at[index[k]], t_buf.at[k], sems.at[0, k]),
                pltpu.make_async_copy(weight, w_buf.at[k], sems.at[1, k]),
            )
        )
    for pair in copies:
        for copy in pair:
            copy.start()
    for k, pair in enumerate(copies):
        for copy in pair:
            copy.wait()
        part = jnp.dot(t_buf[k], w_buf[k], preferred_element_type=jnp.float32)
        total[...] = part if k == 0 else total[...] + part


def early_product(side, index, near, far, near_weights, far_weights):
    weights = near_weights + far_weights
    rows, depth, columns = near.shape[1], near.shape[2], weights[0].shape[1] // 2
    anywhere = pl.BlockSpec(memory_space=pl.ANY)
    count = len(weights)
    return pl.pallas_call(
        functools.partial(early_kernel, len(near_weights), count, side),
        grid_spec=pltpu.PrefetchScalarGridSpec(
            num_scalar_prefetch=1,
            grid=(1,),
            in_specs=[anywhere] * (2 + count),
            out_specs=pl.BlockSpec((rows, columns), lambda i, s: (0, 0)),
            scratch_shapes=[
                pltpu.VMEM((count, depth, columns), jnp.bfloat16),
                pltpu.VMEM((count, rows, depth), jnp.bfloat16),
                pltpu.SemaphoreType.DMA((2, count)),
            ],
        ),
        out_shape=jax.ShapeDtypeStruct((rows, columns), jnp.float32),
        compiler_params=pltpu.CompilerParams(vmem_limit_bytes=LARGE),
        cost_estimate=QUICK,
    )(index, near, far, *weights)


def pick(parts, at):
    return lax.dynamic_index_in_dim(parts, at % 4, 0, keepdims=False)


def product(left, right):
    return jnp.dot(left, right, preferred_element_type=jnp.float32)


def turned_heads(raw, gain, cosine, sine):
    normal = raw * lax.rsqrt(jnp.mean(raw * raw, axis=-1, keepdims=True) + epsilon) * gain
    return normal * cosine + pltpu.roll(normal, HEAD_SIZE // 2, 1) * sine


def heads_kernel(heads, raw_ref, gain, cosine, sine, out_ref):
    for h in range(raw_ref.shape[1] // HEAD_SIZE):
        lanes = slice(h * HEAD_SIZE, (h + 1) * HEAD_SIZE)
        raw = raw_ref[:, lanes]
        if h < heads:
            raw = turned_heads(raw, gain[...], cosine[...], sine[...])
        out_ref[:, lanes] = raw.astype(jnp.bfloat16)


def finish_heads(heads, raw, gain, cosine, sine):
    rows, columns = raw.shape
    step = 256
    block = pl.BlockSpec((step, columns), lambda i: (i, 0))
    table = pl.BlockSpec((step, HEAD_SIZE), lambda i: (i, 0))
    return pl.pallas_call(
        functools.partial(heads_kernel, heads),
        grid=(rows // step,),
        in_specs=[block, pl.BlockSpec((1, HEAD_SIZE), lambda i: (0, 0)), table, table],
        out_specs=block,
        out_shape=jax.ShapeDtypeStruct((rows, columns), jnp.bfloat16),
        compiler_params=pltpu.CompilerParams(vmem_limit_bytes=SMALL),
        cost_estimate=QUICK,
    )(raw, gain, cosine, sine)


def scores_of(queries, keys):
    score = lax.dot_general(
        queries, keys, (((1,), (1,)), ((), ())), preferred_element_type=jnp.float32
    )
    return jnp.exp(score * score_scale)


def lane_sums(weights):
    parts = [weights[:, i : i + HEAD_SIZE] for i in range(0, weights.shape[1], HEAD_SIZE)]
    return functools.reduce(lambda a, b: a + b, parts)


def both_heads(ref, at):
    return jnp.concatenate([ref[at, :HEAD_SIZE], ref[at, HEAD_SIZE:]], axis=0)


def own_kernel(q_ref, k_ref, v_ref, sum_ref, weight_ref):
    for r in range(q_ref.shape[0] // 128):
        at = slice(r * 128, (r + 1) * 128)
        seen = (r + 1) * 128
        e = scores_of(both_heads(q_ref, at), k_ref[:seen])
        i = lax.broadcasted_iota(jnp.int32, e.shape, 0) % 128
        j = lax.broadcasted_iota(jnp.int32, e.shape, 1)
        e = jnp.where(j <= i + r * 128, e, 0.0)
        mixed = jnp.dot(e.astype(jnp.bfloat16), v_ref[:seen], preferred_element_type=jnp.float32)
        weight = lane_sums(e)
        for h in range(2):
            lanes = slice(h * HEAD_SIZE, (h + 1) * HEAD_SIZE)
            sum_ref[at, lanes] = mixed[h * 128 : (h + 1) * 128]
            weight_ref[at, lanes] = weight[h * 128 : (h + 1) * 128]


def behind_kernel(valid, q_ref, k1_ref, v1_ref, k2_ref, v2_ref, sum_ref, weight_ref, out_ref):
    has_one = valid[0].astype(jnp.float32)
    has_two = valid[1].astype(jnp.float32)
    rows = q_ref.shape[0]
    for r in range(rows // 128):
        at = slice(r * 128, (r + 1) * 128)
        q = both_heads(q_ref, at)
        one = scores_of(q, k1_ref[...])
        two = scores_of(q, k2_ref[r * 128 :])
        i = lax.broadcasted_iota(jnp.int32, two.shape, 0) % 128
        j = lax.broadcasted_iota(jnp.int32, two.shape, 1)
        two = jnp.where(j > i, two, 0.0)
        mixed = has_one * jnp.dot(
            one.astype(jnp.bfloat16), v1_ref[...], preferred_element_type=jnp.float32
        ) + has_two * jnp.dot(
            two.astype(jnp.bfloat16), v2_ref[r * 128 :], preferred_element_type=jnp.float32
        )
        weight = has_one * lane_sums(one) + has_two * lane_sums(two)
        for h in range(2):
            lanes = slice(h * HEAD_SIZE, (h + 1) * HEAD_SIZE)
            top = sum_ref[at, lanes] + mixed[h * 128 : (h + 1) * 128]
            low = jnp.sum(weight_ref[at, lanes] + weight[h * 128 : (h + 1) * 128], axis=-1, keepdims=True)
            out_ref[at, lanes] = (top / low).astype(jnp.bfloat16)


def attend_own(queries, keyed):
    rows, columns = queries.shape
    groups = columns // (2 * HEAD_SIZE)
    pair = pl.BlockSpec((rows, 2 * HEAD_SIZE), lambda g: (0, g))
    shape = jax.ShapeDtypeStruct((rows, columns), jnp.float32)
    return pl.pallas_call(
        own_kernel,
        grid=(groups,),
        in_specs=[
            pair,
            pl.BlockSpec((rows, HEAD_SIZE), lambda g: (0, g)),
            pl.BlockSpec((rows, HEAD_SIZE), lambda g: (0, groups + g)),
        ],
        out_specs=[pair, pair],
        out_shape=[shape, shape],
        compiler_params=pltpu.CompilerParams(vmem_limit_bytes=SMALL),
        cost_estimate=QUICK,
    )(queries, keyed, keyed)


def attend_behind(valid, queries, one, two, sums, weights):
    rows, columns = queries.shape
    groups = columns // (2 * HEAD_SIZE)
    pair = pl.BlockSpec((rows, 2 * HEAD_SIZE), lambda g, s: (0, g))
    keys = pl.BlockSpec((rows, HEAD_SIZE), lambda g, s: (0, g))
    values = pl.BlockSpec((rows, HEAD_SIZE), lambda g, s: (0, groups + g))
    return pl.pallas_call(
        behind_kernel,
        grid_spec=pltpu.PrefetchScalarGridSpec(
            num_scalar_prefetch=1,
            grid=(groups,),
            in_specs=[pair, keys, values, keys, values, pair, pair],
            out_specs=pair,
        ),
        out_shape=jax.ShapeDtypeStruct((rows, columns), jnp.bfloat16),
        compiler_params=pltpu.CompilerParams(vmem_limit_bytes=SMALL),
        cost_estimate=QUICK,
    )(valid, queries, one, one, two, two, sums, weights)


def half_kernel(half, weight_ref, context_ref, out_ref):
    out_ref[...] = lax.dot_general(
        weight_ref[...], context_ref[...], (((1,), (1,)), ((), ())), preferred_element_type=jnp.float32
    ).astype(out_ref.dtype)


def out_half(weight, context, half, dtype):
    rows, depth = context.shape
    columns = weight.shape[0] // 2
    steps = 4
    tile = columns // steps
    return pl.pallas_call(
        half_kernel,
        grid_spec=pltpu.PrefetchScalarGridSpec(
            num_scalar_prefetch=1,
            grid=(steps,),
            in_specs=[
                pl.BlockSpec((tile, depth), lambda i, s: (s[0] * steps + i, 0)),
                pl.BlockSpec((rows, depth), lambda i, s: (0, 0)),
            ],
            out_specs=pl.BlockSpec((tile, rows), lambda i, s: (i, 0)),
        ),
        out_shape=jax.ShapeDtypeStruct((columns, rows), dtype),
        compiler_params=pltpu.CompilerParams(vmem_limit_bytes=SMALL),
        cost_estimate=QUICK,
    )(half[None], weight, context)


def local(
    tokens, q_weight, key_matrix, value_matrix, o_weight, pre_gain, post_gain, q_gain, k_gain
):
    rows = tokens.shape[0]
    q_cols = q_weight.shape[1]
    yl, x, z, yh, c = (lax.axis_index(name) for name in ("yl", "x", "z", "yh", "c"))
    seq_index = (yl * 4 + x) * 4 + z
    whole = lax.all_gather(tokens.T, MP, axis=0)

    own = beside(q_weight, key_matrix, value_matrix)
    other = shift(own, "yl", 1)
    own_pieces = [own] + [shift(own, "x", step) for step in (1, 3, 2)]
    other_pieces = [other] + [shift(other, "z", step) for step in (1, 3, 2)]
    own_line = in_line(own_pieces, x)
    other_line = in_line(other_pieces, z)
    own_line, turned = lax.optimization_barrier((own_line, o_weight.T))
    own_ahead, own_behind = shift(own_line, "z", 1), shift(own_line, "z", 3)
    other_ahead, other_behind = shift(other_line, "x", 1), shift(other_line, "x", 3)
    near, far = norm_parts(whole, pre_gain, yl)

    y = yh * 2 + yl
    flat = lambda p: (p % 2) * 2 + p // 2
    one = lax.ppermute(turned, ("yl", "yh"), [(flat(a), flat(b)) for a, b in ((0, 1), (2, 0), (1, 3), (3, 2))])
    two = lax.ppermute(turned, ("yl", "yh"), [(flat(a), flat(b)) for a, b in ((1, 2), (2, 1))])
    positions = seq_index * rows + jnp.arange(rows, dtype=jnp.int32)
    half = HEAD_SIZE // 2
    freq = 10000.0 ** (-(jnp.arange(half, dtype=jnp.float32) * 2.0) / HEAD_SIZE)
    angle = positions.astype(jnp.float32)[:, None] * freq[None, :]
    cosine = jnp.cos(angle)
    sine = jnp.sin(angle)
    cosine = jnp.concatenate([cosine, cosine], axis=1)
    sine = jnp.concatenate([-sine, sine], axis=1)
    index = jnp.stack([z, (z + 3) % 4, (z + 1) % 4, x, (x + 3) % 4, (x + 1) % 4])

    own_ahead, own_behind, other_ahead, other_behind, near, far, one, two, cosine, sine, index = (
        lax.optimization_barrier(
            (own_ahead, own_behind, other_ahead, other_behind, near, far, one, two, cosine, sine, index)
        )
    )

    own_far_kv = shift(cut(own_behind, 1), "z", 3)
    other_far_kv = shift(cut(other_behind, 1), "x", 3)
    own_far_q = shift(cut(own_ahead, 0), "z", 1)
    other_far_q = shift(cut(other_ahead, 0), "x", 1)
    outer = (y == 0) | (y == 3)
    pair = jnp.concatenate([jnp.where(outer, turned, one), jnp.where(outer, one, two)], axis=1)
    out_all = lax.all_gather(pair, ("x", "z"), axis=0, tiled=True)
    parts = [own_line, own_ahead, own_behind], [other_line, other_ahead, other_behind]
    part_kv = early_product(1, index, near, far, *parts)
    part_kv, own_far_kv, other_far_kv = lax.optimization_barrier((part_kv, own_far_kv, other_far_kv))


    part_kv = part_kv + product(pick(near, z + 2), own_far_kv) + product(pick(far, x + 2), other_far_kv)
    keyed = finish_heads(2, part_kv, k_gain[None], cosine, sine)
    behind_one = from_behind(keyed, 1)
    behind_two = from_behind(keyed, 2)
    keyed, index = lax.optimization_barrier((keyed, index))
    part_q = early_product(0, index, near, far, *parts)
    part_q = part_q + product(pick(near, z + 2), own_far_q) + product(pick(far, x + 2), other_far_q)
    queries = finish_heads(4, part_q, q_gain[None], cosine, sine)
    sums, weights = attend_own(queries, keyed)
    valid = jnp.stack([seq_index >= 1, seq_index >= 2]).astype(jnp.int32)
    context = attend_behind(valid, queries, behind_one, behind_two, sums, weights)
    across = shift(context, "yh", 1)
    out_all, context = lax.optimization_barrier((out_all, context))
    both = jnp.concatenate([context, across], axis=1)

    half_of = functools.partial(out_half, out_all, both)
    received = shift(half_of(1 - c, jnp.bfloat16), "c", 1)
    kept, received = lax.optimization_barrier((half_of(c, jnp.float32), received))
    share = (kept + received.astype(jnp.float32)).T
    squares = jnp.sum(share * share, axis=1)
    others = [lax.ppermute(squares, MP, [(i, i ^ bit) for i in range(4)]) for bit in (2, 3, 1)]
    total = (squares + others[2]) + (others[0] + others[1])
    scale_rows = lax.rsqrt(total / MODEL_WIDTH + epsilon)
    return (tokens.astype(jnp.float32) + share * scale_rows[:, None] * post_gain).astype(
        jnp.bfloat16
    )


def solution(mesh):
    fine = Mesh(np.asarray(mesh.devices).reshape(2, 4, 4, 2, 2), SEQ + MP)
    return jax.shard_map(
        local,
        mesh=fine,
        in_specs=(
            P(SEQ, MP),
            P(SEQ, MP),
            P(SEQ, MP),
            P(SEQ, MP),
            P(MP, SEQ),
            P(),
            P(MP),
            P(),
            P(),
        ),
        out_specs=P(SEQ, MP),
        check_vma=False,
    )
```

```python
import functools

import jax
import jax.numpy as jnp
import numpy as np
from jax import lax
from jax.experimental import pallas as pl
from jax.experimental.pallas import tpu as pltpu
from jax.sharding import Mesh, PartitionSpec as P

MODEL_WIDTH = 5376
HEAD_SIZE = 128
WINDOW_LENGTH = 1024
SHARD = MODEL_WIDTH // 32
VMEM = 40 << 20
SMALL = 16 << 20
LARGE = 58 << 20
QUICK = pl.CostEstimate(flops=0, bytes_accessed=0, transcendentals=0)

score_scale = 168.0 ** (-0.5)
epsilon = 1e-06
SEQ = ("yl", "x", "z")
MP = ("yh", "c")


def shift(value, axis, step):
    count = lax.axis_size(axis)
    return lax.ppermute(value, axis, [(i, (i + step) % count) for i in range(count)])


def from_behind(value, steps):
    count = 32
    return lax.ppermute(value, SEQ, [(source, source + steps) for source in range(count - steps)])


def later(values, done):
    return lax.optimization_barrier((values, done))[0]


def line_kernel(slots, *refs):
    for k, piece in enumerate(refs[:4]):

        @pl.when(pl.program_id(0) == k)
        def _():
            refs[4][0] = piece[...]


def in_line(pieces, at):
    depth, columns = pieces[0].shape
    line = pl.pallas_call(
        line_kernel,
        grid_spec=pltpu.PrefetchScalarGridSpec(
            num_scalar_prefetch=1,
            grid=(4,),
            in_specs=[pl.BlockSpec((depth, columns), lambda i, s: (0, 0))] * 4,
            out_specs=pl.BlockSpec((1, depth, columns), lambda i, s: (s[i], 0, 0)),
        ),
        out_shape=jax.ShapeDtypeStruct((4, depth, columns), jnp.bfloat16),
        compiler_params=pltpu.CompilerParams(vmem_limit_bytes=VMEM),
        cost_estimate=QUICK,
    )((at + jnp.array([0, 3, 1, 2], jnp.int32)) % 4, *pieces)
    return line.reshape(4 * depth, columns)


def beside_kernel(*refs):
    out_ref, start = refs[-1], 0
    for ref in refs[:-1]:
        out_ref[:, start : start + ref.shape[1]] = ref[...]
        start += ref.shape[1]


def beside(*values):
    rows, columns = values[0].shape[0], sum(value.shape[1] for value in values)
    return pl.pallas_call(
        beside_kernel,
        out_shape=jax.ShapeDtypeStruct((rows, columns), values[0].dtype),
        compiler_params=pltpu.CompilerParams(vmem_limit_bytes=LARGE),
        cost_estimate=QUICK,
    )(*values)


def cut_kernel(value_ref, out_ref):
    out_ref[...] = value_ref[...]


def cut(value, part):
    rows, columns = value.shape
    step = rows // 2
    return pl.pallas_call(
        cut_kernel,
        grid=(2,),
        in_specs=[pl.BlockSpec((step, columns // 2), lambda i: (i, part))],
        out_specs=pl.BlockSpec((step, columns // 2), lambda i: (i, 0)),
        out_shape=jax.ShapeDtypeStruct((rows, columns // 2), value.dtype),
        compiler_params=pltpu.CompilerParams(vmem_limit_bytes=VMEM),
        cost_estimate=QUICK,
    )(value)


def norm_kernel(side, own_ref, other_ref, near_gain, far_gain, near_ref, far_ref):
    own = own_ref[0].astype(jnp.float32)
    other = other_ref[0].astype(jnp.float32)
    total = jnp.sum(own * own, axis=(0, 1)) + jnp.sum(other * other, axis=(0, 1))
    scale = lax.rsqrt(total / MODEL_WIDTH + epsilon)[None, None]
    own = own * scale
    other = other * scale
    for i in range(4):
        starts = [(j // 2, ((j % 2) * 4 + i) * SHARD) for j in range(4)]
        part = jnp.concatenate([own[k, s : s + SHARD] for k, s in starts], axis=0)
        near_ref[i] = (part.T * near_gain[0, i]).astype(jnp.bfloat16)
        start = (i % 2) * 4 * SHARD
        part = other[i // 2, start : start + 4 * SHARD]
        far_ref[i] = (part.T * far_gain[0, i]).astype(jnp.bfloat16)


def norm_parts(pieces, gain, side):
    width, rows = pieces.shape[1:]
    step = 256
    pieces = pieces.reshape(2, 2, width, rows)
    far_gain = gain.reshape(2, 4, 4, SHARD)
    near_gain = jnp.swapaxes(far_gain, 1, 2).reshape(2, 4, 1, 4 * SHARD)
    far_gain = far_gain.reshape(2, 4, 1, 4 * SHARD)
    half = lambda flip: pl.BlockSpec((1, 2, width, step), lambda i, s: (s[flip], 0, 0, i))
    gains = lambda flip: pl.BlockSpec((1, 4, 1, 4 * SHARD), lambda i, s: (s[flip], 0, 0, 0))
    out = pl.BlockSpec((4, step, 4 * SHARD), lambda i, s: (0, i, 0))
    shape = jax.ShapeDtypeStruct((4, rows, 4 * SHARD), jnp.bfloat16)
    return pl.pallas_call(
        norm_kernel,
        grid_spec=pltpu.PrefetchScalarGridSpec(
            num_scalar_prefetch=1,
            grid=(rows // step,),
            in_specs=[half(0), half(1), gains(0), gains(1)],
            out_specs=[out, out],
        ),
        out_shape=[shape, shape],
        compiler_params=pltpu.CompilerParams(vmem_limit_bytes=LARGE),
        cost_estimate=QUICK,
    )(jnp.stack([side, 1 - side]), pieces, pieces, near_gain, far_gain)


def early_kernel(n_near, count, side, index, near_ref, far_ref, *refs):
    weights, (total, w_buf, t_buf, sems) = refs[:count], refs[count:]
    columns = total.shape[1]
    copies = []
    for k in range(count):
        source = near_ref if k < n_near else far_ref
        weight = weights[k].at[:, side * columns : (side + 1) * columns]
        copies.append(
            (
                pltpu.make_async_copy(source.at[index[k]], t_buf.at[k], sems.at[0, k]),
                pltpu.make_async_copy(weight, w_buf.at[k], sems.at[1, k]),
            )
        )
    for pair in copies:
        for copy in pair:
            copy.start()
    for k, pair in enumerate(copies):
        for copy in pair:
            copy.wait()
        part = jnp.dot(t_buf[k], w_buf[k], preferred_element_type=jnp.float32)
        total[...] = part if k == 0 else total[...] + part


def early_product(side, index, near, far, near_weights, far_weights):
    weights = near_weights + far_weights
    rows, depth, columns = near.shape[1], near.shape[2], weights[0].shape[1] // 2
    anywhere = pl.BlockSpec(memory_space=pl.ANY)
    count = len(weights)
    return pl.pallas_call(
        functools.partial(early_kernel, len(near_weights), count, side),
        grid_spec=pltpu.PrefetchScalarGridSpec(
            num_scalar_prefetch=1,
            grid=(1,),
            in_specs=[anywhere] * (2 + count),
            out_specs=pl.BlockSpec((rows, columns), lambda i, s: (0, 0)),
            scratch_shapes=[
                pltpu.VMEM((count, depth, columns), jnp.bfloat16),
                pltpu.VMEM((count, rows, depth), jnp.bfloat16),
                pltpu.SemaphoreType.DMA((2, count)),
            ],
        ),
        out_shape=jax.ShapeDtypeStruct((rows, columns), jnp.float32),
        compiler_params=pltpu.CompilerParams(vmem_limit_bytes=LARGE),
        cost_estimate=QUICK,
    )(index, near, far, *weights)


def pick(parts, at):
    return lax.dynamic_index_in_dim(parts, at % 4, 0, keepdims=False)


def product(left, right):
    return jnp.dot(left, right, preferred_element_type=jnp.float32)


def turned_heads(raw, gain, cosine, sine):
    normal = raw * lax.rsqrt(jnp.mean(raw * raw, axis=-1, keepdims=True) + epsilon) * gain
    return normal * cosine + pltpu.roll(normal, HEAD_SIZE // 2, 1) * sine


def heads_kernel(heads, raw_ref, gain, cosine, sine, out_ref):
    for h in range(raw_ref.shape[1] // HEAD_SIZE):
        lanes = slice(h * HEAD_SIZE, (h + 1) * HEAD_SIZE)
        raw = raw_ref[:, lanes]
        if h < heads:
            raw = turned_heads(raw, gain[...], cosine[...], sine[...])
        out_ref[:, lanes] = raw.astype(jnp.bfloat16)


def finish_heads(heads, raw, gain, cosine, sine):
    rows, columns = raw.shape
    step = 256
    block = pl.BlockSpec((step, columns), lambda i: (i, 0))
    table = pl.BlockSpec((step, HEAD_SIZE), lambda i: (i, 0))
    return pl.pallas_call(
        functools.partial(heads_kernel, heads),
        grid=(rows // step,),
        in_specs=[block, pl.BlockSpec((1, HEAD_SIZE), lambda i: (0, 0)), table, table],
        out_specs=block,
        out_shape=jax.ShapeDtypeStruct((rows, columns), jnp.bfloat16),
        compiler_params=pltpu.CompilerParams(vmem_limit_bytes=SMALL),
        cost_estimate=QUICK,
    )(raw, gain, cosine, sine)


def scores_of(queries, keys):
    score = lax.dot_general(
        queries, keys, (((1,), (1,)), ((), ())), preferred_element_type=jnp.float32
    )
    return jnp.exp(score * score_scale)


def lane_sums(weights):
    parts = [weights[:, i : i + HEAD_SIZE] for i in range(0, weights.shape[1], HEAD_SIZE)]
    return functools.reduce(lambda a, b: a + b, parts)


def both_heads(ref, at):
    return jnp.concatenate([ref[at, :HEAD_SIZE], ref[at, HEAD_SIZE:]], axis=0)


def own_kernel(q_ref, k_ref, v_ref, sum_ref, weight_ref):
    for r in range(q_ref.shape[0] // 128):
        at = slice(r * 128, (r + 1) * 128)
        seen = (r + 1) * 128
        e = scores_of(both_heads(q_ref, at), k_ref[:seen])
        i = lax.broadcasted_iota(jnp.int32, e.shape, 0) % 128
        j = lax.broadcasted_iota(jnp.int32, e.shape, 1)
        e = jnp.where(j <= i + r * 128, e, 0.0)
        mixed = jnp.dot(e.astype(jnp.bfloat16), v_ref[:seen], preferred_element_type=jnp.float32)
        weight = lane_sums(e)
        for h in range(2):
            lanes = slice(h * HEAD_SIZE, (h + 1) * HEAD_SIZE)
            sum_ref[at, lanes] = mixed[h * 128 : (h + 1) * 128]
            weight_ref[at, lanes] = weight[h * 128 : (h + 1) * 128]


def behind_kernel(valid, q_ref, k1_ref, v1_ref, k2_ref, v2_ref, sum_ref, weight_ref, out_ref):
    has_one = valid[0].astype(jnp.float32)
    has_two = valid[1].astype(jnp.float32)
    rows = q_ref.shape[0]
    for r in range(rows // 128):
        at = slice(r * 128, (r + 1) * 128)
        q = both_heads(q_ref, at)
        one = scores_of(q, k1_ref[...])
        two = scores_of(q, k2_ref[r * 128 :])
        i = lax.broadcasted_iota(jnp.int32, two.shape, 0) % 128
        j = lax.broadcasted_iota(jnp.int32, two.shape, 1)
        two = jnp.where(j > i, two, 0.0)
        mixed = has_one * jnp.dot(
            one.astype(jnp.bfloat16), v1_ref[...], preferred_element_type=jnp.float32
        ) + has_two * jnp.dot(
            two.astype(jnp.bfloat16), v2_ref[r * 128 :], preferred_element_type=jnp.float32
        )
        weight = has_one * lane_sums(one) + has_two * lane_sums(two)
        for h in range(2):
            lanes = slice(h * HEAD_SIZE, (h + 1) * HEAD_SIZE)
            top = sum_ref[at, lanes] + mixed[h * 128 : (h + 1) * 128]
            low = jnp.sum(weight_ref[at, lanes] + weight[h * 128 : (h + 1) * 128], axis=-1, keepdims=True)
            out_ref[at, lanes] = (top / low).astype(jnp.bfloat16)


def attend_own(queries, keyed):
    rows, columns = queries.shape
    groups = columns // (2 * HEAD_SIZE)
    pair = pl.BlockSpec((rows, 2 * HEAD_SIZE), lambda g: (0, g))
    shape = jax.ShapeDtypeStruct((rows, columns), jnp.float32)
    return pl.pallas_call(
        own_kernel,
        grid=(groups,),
        in_specs=[
            pair,
            pl.BlockSpec((rows, HEAD_SIZE), lambda g: (0, g)),
            pl.BlockSpec((rows, HEAD_SIZE), lambda g: (0, groups + g)),
        ],
        out_specs=[pair, pair],
        out_shape=[shape, shape],
        compiler_params=pltpu.CompilerParams(vmem_limit_bytes=SMALL),
        cost_estimate=QUICK,
    )(queries, keyed, keyed)


def attend_behind(valid, queries, one, two, sums, weights):
    rows, columns = queries.shape
    groups = columns // (2 * HEAD_SIZE)
    pair = pl.BlockSpec((rows, 2 * HEAD_SIZE), lambda g, s: (0, g))
    keys = pl.BlockSpec((rows, HEAD_SIZE), lambda g, s: (0, g))
    values = pl.BlockSpec((rows, HEAD_SIZE), lambda g, s: (0, groups + g))
    return pl.pallas_call(
        behind_kernel,
        grid_spec=pltpu.PrefetchScalarGridSpec(
            num_scalar_prefetch=1,
            grid=(groups,),
            in_specs=[pair, keys, values, keys, values, pair, pair],
            out_specs=pair,
        ),
        out_shape=jax.ShapeDtypeStruct((rows, columns), jnp.bfloat16),
        compiler_params=pltpu.CompilerParams(vmem_limit_bytes=SMALL),
        cost_estimate=QUICK,
    )(valid, queries, one, one, two, two, sums, weights)


def half_kernel(half, weight_ref, context_ref, out_ref):
    out_ref[...] = lax.dot_general(
        weight_ref[...], context_ref[...], (((1,), (1,)), ((), ())), preferred_element_type=jnp.float32
    ).astype(out_ref.dtype)


def out_half(weight, context, half, dtype):
    rows, depth = context.shape
    columns = weight.shape[0] // 2
    steps = 4
    tile = columns // steps
    return pl.pallas_call(
        half_kernel,
        grid_spec=pltpu.PrefetchScalarGridSpec(
            num_scalar_prefetch=1,
            grid=(steps,),
            in_specs=[
                pl.BlockSpec((tile, depth), lambda i, s: (s[0] * steps + i, 0)),
                pl.BlockSpec((rows, depth), lambda i, s: (0, 0)),
            ],
            out_specs=pl.BlockSpec((tile, rows), lambda i, s: (i, 0)),
        ),
        out_shape=jax.ShapeDtypeStruct((columns, rows), dtype),
        compiler_params=pltpu.CompilerParams(vmem_limit_bytes=SMALL),
        cost_estimate=QUICK,
    )(half[None], weight, context)


def local(
    tokens, q_weight, key_matrix, value_matrix, o_weight, pre_gain, post_gain, q_gain, k_gain
):
    rows = tokens.shape[0]
    q_cols = q_weight.shape[1]
    yl, x, z, yh, c = (lax.axis_index(name) for name in ("yl", "x", "z", "yh", "c"))
    seq_index = (yl * 4 + x) * 4 + z
    whole = lax.all_gather(tokens.T, MP, axis=0)

    own = beside(q_weight, key_matrix, value_matrix)
    other = shift(own, "yl", 1)
    own_pieces = [own] + [shift(own, "x", step) for step in (1, 3, 2)]
    other_pieces = [other] + [shift(other, "z", step) for step in (1, 3, 2)]
    own_line = in_line(own_pieces, x)
    other_line = in_line(other_pieces, z)
    own_line, turned = lax.optimization_barrier((own_line, o_weight.T))
    own_ahead, own_behind = shift(own_line, "z", 1), shift(own_line, "z", 3)
    other_ahead, other_behind = shift(other_line, "x", 1), shift(other_line, "x", 3)
    near, far = norm_parts(whole, pre_gain, yl)

    y = yh * 2 + yl
    flat = lambda p: (p % 2) * 2 + p // 2
    one = lax.ppermute(turned, ("yl", "yh"), [(flat(a), flat(b)) for a, b in ((0, 1), (2, 0), (1, 3), (3, 2))])
    two = lax.ppermute(turned, ("yl", "yh"), [(flat(a), flat(b)) for a, b in ((1, 2), (2, 1))])
    positions = seq_index * rows + jnp.arange(rows, dtype=jnp.int32)
    half = HEAD_SIZE // 2
    freq = 10000.0 ** (-(jnp.arange(half, dtype=jnp.float32) * 2.0) / HEAD_SIZE)
    angle = positions.astype(jnp.float32)[:, None] * freq[None, :]
    cosine = jnp.cos(angle)
    sine = jnp.sin(angle)
    cosine = jnp.concatenate([cosine, cosine], axis=1)
    sine = jnp.concatenate([-sine, sine], axis=1)
    index = jnp.stack([z, (z + 3) % 4, (z + 1) % 4, x, (x + 3) % 4, (x + 1) % 4])

    own_ahead, own_behind, other_ahead, other_behind, near, far, one, two, cosine, sine, index = (
        lax.optimization_barrier(
            (own_ahead, own_behind, other_ahead, other_behind, near, far, one, two, cosine, sine, index)
        )
    )

    own_far_kv = shift(cut(own_behind, 1), "z", 3)
    other_far_kv = shift(cut(other_behind, 1), "x", 3)
    own_far_q = shift(cut(own_ahead, 0), "z", 1)
    other_far_q = shift(cut(other_ahead, 0), "x", 1)
    outer = (y == 0) | (y == 3)
    pair = jnp.concatenate([jnp.where(outer, turned, one), jnp.where(outer, one, two)], axis=1)
    out_all = lax.all_gather(pair, ("x", "z"), axis=0, tiled=True)
    parts = [own_line, own_ahead, own_behind], [other_line, other_ahead, other_behind]
    part_kv = early_product(1, index, near, far, *parts)
    part_kv, own_far_kv, other_far_kv = lax.optimization_barrier((part_kv, own_far_kv, other_far_kv))


    part_kv = part_kv + product(pick(near, z + 2), own_far_kv) + product(pick(far, x + 2), other_far_kv)
    keyed = finish_heads(2, part_kv, k_gain[None], cosine, sine)
    behind_one = from_behind(keyed, 1)
    behind_two = from_behind(keyed, 2)
    keyed, index = lax.optimization_barrier((keyed, index))
    part_q = early_product(0, index, near, far, *parts)
    part_q = part_q + product(pick(near, z + 2), own_far_q) + product(pick(far, x + 2), other_far_q)
    queries = finish_heads(4, part_q, q_gain[None], cosine, sine)
    sums, weights = attend_own(queries, keyed)
    valid = jnp.stack([seq_index >= 1, seq_index >= 2]).astype(jnp.int32)
    context = attend_behind(valid, queries, behind_one, behind_two, sums, weights)
    across = shift(context, "yh", 1)
    out_all, context = lax.optimization_barrier((out_all, context))
    both = jnp.concatenate([context, across], axis=1)

    half_of = functools.partial(out_half, out_all, both)
    received = shift(half_of(1 - c, jnp.bfloat16), "c", 1)
    kept, received = lax.optimization_barrier((half_of(c, jnp.float32), received))
    share = (kept + received.astype(jnp.float32)).T
    squares = jnp.sum(share * share, axis=1)
    squares = squares + shift(squares, "c", 1)
    total = squares + shift(squares, "yh", 1)
    scale_rows = lax.rsqrt(total / MODEL_WIDTH + epsilon)
    return (tokens.astype(jnp.float32) + share * scale_rows[:, None] * post_gain).astype(
        jnp.bfloat16
    )


def solution(mesh):
    fine = Mesh(np.asarray(mesh.devices).reshape(2, 4, 4, 2, 2), SEQ + MP)
    return jax.shard_map(
        local,
        mesh=fine,
        in_specs=(
            P(SEQ, MP),
            P(SEQ, MP),
            P(SEQ, MP),
            P(SEQ, MP),
            P(MP, SEQ),
            P(),
            P(MP),
            P(),
            P(),
        ),
        out_specs=P(SEQ, MP),
        check_vma=False,
    )
```

```python
import functools

import jax
import jax.numpy as jnp
import numpy as np
from jax import lax
from jax.experimental import pallas as pl
from jax.experimental.pallas import tpu as pltpu
from jax.sharding import Mesh, PartitionSpec as P

MODEL_WIDTH = 5376
HEAD_SIZE = 128
WINDOW_LENGTH = 1024
SHARD = MODEL_WIDTH // 32
VMEM = 40 << 20
SMALL = 16 << 20
LARGE = 58 << 20
QUICK = pl.CostEstimate(flops=0, bytes_accessed=0, transcendentals=0)

score_scale = 168.0 ** (-0.5)
epsilon = 1e-06
SEQ = ("yl", "x", "z")
MP = ("yh", "c")


def shift(value, axis, step):
    count = lax.axis_size(axis)
    return lax.ppermute(value, axis, [(i, (i + step) % count) for i in range(count)])


def from_behind(value, steps):
    count = 32
    return lax.ppermute(value, SEQ, [(source, source + steps) for source in range(count - steps)])


def later(values, done):
    return lax.optimization_barrier((values, done))[0]


def line_kernel(slots, *refs):
    for k, piece in enumerate(refs[:4]):

        @pl.when(pl.program_id(0) == k)
        def _():
            refs[4][0] = piece[...]


def in_line(pieces, at):
    depth, columns = pieces[0].shape
    line = pl.pallas_call(
        line_kernel,
        grid_spec=pltpu.PrefetchScalarGridSpec(
            num_scalar_prefetch=1,
            grid=(4,),
            in_specs=[pl.BlockSpec((depth, columns), lambda i, s: (0, 0))] * 4,
            out_specs=pl.BlockSpec((1, depth, columns), lambda i, s: (s[i], 0, 0)),
        ),
        out_shape=jax.ShapeDtypeStruct((4, depth, columns), jnp.bfloat16),
        compiler_params=pltpu.CompilerParams(vmem_limit_bytes=VMEM),
        cost_estimate=QUICK,
    )((at + jnp.array([0, 3, 1, 2], jnp.int32)) % 4, *pieces)
    return line.reshape(4 * depth, columns)


def beside_kernel(*refs):
    out_ref, start = refs[-1], 0
    for ref in refs[:-1]:
        out_ref[:, start : start + ref.shape[1]] = ref[...]
        start += ref.shape[1]


def beside(*values):
    rows, columns = values[0].shape[0], sum(value.shape[1] for value in values)
    return pl.pallas_call(
        beside_kernel,
        out_shape=jax.ShapeDtypeStruct((rows, columns), values[0].dtype),
        compiler_params=pltpu.CompilerParams(vmem_limit_bytes=LARGE),
        cost_estimate=QUICK,
    )(*values)


def cut_kernel(value_ref, out_ref):
    out_ref[...] = value_ref[...]


def cut(value, part):
    rows, columns = value.shape
    step = rows // 2
    return pl.pallas_call(
        cut_kernel,
        grid=(2,),
        in_specs=[pl.BlockSpec((step, columns // 2), lambda i: (i, part))],
        out_specs=pl.BlockSpec((step, columns // 2), lambda i: (i, 0)),
        out_shape=jax.ShapeDtypeStruct((rows, columns // 2), value.dtype),
        compiler_params=pltpu.CompilerParams(vmem_limit_bytes=VMEM),
        cost_estimate=QUICK,
    )(value)


def norm_kernel(side, own_ref, other_ref, near_gain, far_gain, near_ref, far_ref):
    own = own_ref[0].astype(jnp.float32)
    other = other_ref[0].astype(jnp.float32)
    total = jnp.sum(own * own, axis=(0, 1)) + jnp.sum(other * other, axis=(0, 1))
    scale = lax.rsqrt(total / MODEL_WIDTH + epsilon)[None, None]
    own = own * scale
    other = other * scale
    for i in range(4):
        starts = [(j // 2, ((j % 2) * 4 + i) * SHARD) for j in range(4)]
        part = jnp.concatenate([own[k, s : s + SHARD] for k, s in starts], axis=0)
        near_ref[i] = (part.T * near_gain[0, i]).astype(jnp.bfloat16)
        start = (i % 2) * 4 * SHARD
        part = other[i // 2, start : start + 4 * SHARD]
        far_ref[i] = (part.T * far_gain[0, i]).astype(jnp.bfloat16)


def norm_parts(pieces, gain, side):
    width, rows = pieces.shape[1:]
    step = 256
    pieces = pieces.reshape(2, 2, width, rows)
    far_gain = gain.reshape(2, 4, 4, SHARD)
    near_gain = jnp.swapaxes(far_gain, 1, 2).reshape(2, 4, 1, 4 * SHARD)
    far_gain = far_gain.reshape(2, 4, 1, 4 * SHARD)
    half = lambda flip: pl.BlockSpec((1, 2, width, step), lambda i, s: (s[flip], 0, 0, i))
    gains = lambda flip: pl.BlockSpec((1, 4, 1, 4 * SHARD), lambda i, s: (s[flip], 0, 0, 0))
    out = pl.BlockSpec((4, step, 4 * SHARD), lambda i, s: (0, i, 0))
    shape = jax.ShapeDtypeStruct((4, rows, 4 * SHARD), jnp.bfloat16)
    return pl.pallas_call(
        norm_kernel,
        grid_spec=pltpu.PrefetchScalarGridSpec(
            num_scalar_prefetch=1,
            grid=(rows // step,),
            in_specs=[half(0), half(1), gains(0), gains(1)],
            out_specs=[out, out],
        ),
        out_shape=[shape, shape],
        compiler_params=pltpu.CompilerParams(vmem_limit_bytes=LARGE),
        cost_estimate=QUICK,
    )(jnp.stack([side, 1 - side]), pieces, pieces, near_gain, far_gain)


def early_kernel(n_near, count, side, index, near_ref, far_ref, *refs):
    weights, (total, w_buf, t_buf, sems) = refs[:count], refs[count:]
    columns = total.shape[1]
    copies = []
    for k in range(count):
        source = near_ref if k < n_near else far_ref
        weight = weights[k].at[:, side * columns : (side + 1) * columns]
        copies.append(
            (
                pltpu.make_async_copy(source.at[index[k]], t_buf.at[k], sems.at[0, k]),
                pltpu.make_async_copy(weight, w_buf.at[k], sems.at[1, k]),
            )
        )
    for pair in copies:
        for copy in pair:
            copy.start()
    for k, pair in enumerate(copies):
        for copy in pair:
            copy.wait()
        part = jnp.dot(t_buf[k], w_buf[k], preferred_element_type=jnp.float32)
        total[...] = part if k == 0 else total[...] + part


def early_product(side, index, near, far, near_weights, far_weights):
    weights = near_weights + far_weights
    rows, depth, columns = near.shape[1], near.shape[2], weights[0].shape[1] // 2
    anywhere = pl.BlockSpec(memory_space=pl.ANY)
    count = len(weights)
    return pl.pallas_call(
        functools.partial(early_kernel, len(near_weights), count, side),
        grid_spec=pltpu.PrefetchScalarGridSpec(
            num_scalar_prefetch=1,
            grid=(1,),
            in_specs=[anywhere] * (2 + count),
            out_specs=pl.BlockSpec((rows, columns), lambda i, s: (0, 0)),
            scratch_shapes=[
                pltpu.VMEM((count, depth, columns), jnp.bfloat16),
                pltpu.VMEM((count, rows, depth), jnp.bfloat16),
                pltpu.SemaphoreType.DMA((2, count)),
            ],
        ),
        out_shape=jax.ShapeDtypeStruct((rows, columns), jnp.float32),
        compiler_params=pltpu.CompilerParams(vmem_limit_bytes=LARGE),
        cost_estimate=QUICK,
    )(index, near, far, *weights)


def pick(parts, at):
    return lax.dynamic_index_in_dim(parts, at % 4, 0, keepdims=False)


def product(left, right):
    return jnp.dot(left, right, preferred_element_type=jnp.float32)


def turned_heads(raw, gain, cosine, sine):
    normal = raw * lax.rsqrt(jnp.mean(raw * raw, axis=-1, keepdims=True) + epsilon) * gain
    return normal * cosine + pltpu.roll(normal, HEAD_SIZE // 2, 1) * sine


def heads_kernel(heads, raw_ref, gain, cosine, sine, out_ref):
    for h in range(raw_ref.shape[1] // HEAD_SIZE):
        lanes = slice(h * HEAD_SIZE, (h + 1) * HEAD_SIZE)
        raw = raw_ref[:, lanes]
        if h < heads:
            raw = turned_heads(raw, gain[...], cosine[...], sine[...])
        out_ref[:, lanes] = raw.astype(jnp.bfloat16)


def finish_heads(heads, raw, gain, cosine, sine):
    rows, columns = raw.shape
    step = 256
    block = pl.BlockSpec((step, columns), lambda i: (i, 0))
    table = pl.BlockSpec((step, HEAD_SIZE), lambda i: (i, 0))
    return pl.pallas_call(
        functools.partial(heads_kernel, heads),
        grid=(rows // step,),
        in_specs=[block, pl.BlockSpec((1, HEAD_SIZE), lambda i: (0, 0)), table, table],
        out_specs=block,
        out_shape=jax.ShapeDtypeStruct((rows, columns), jnp.bfloat16),
        compiler_params=pltpu.CompilerParams(vmem_limit_bytes=SMALL),
        cost_estimate=QUICK,
    )(raw, gain, cosine, sine)


def scores_of(queries, keys):
    score = lax.dot_general(
        queries, keys, (((1,), (1,)), ((), ())), preferred_element_type=jnp.float32
    )
    return jnp.exp(score * score_scale)


def lane_sums(weights):
    parts = [weights[:, i : i + HEAD_SIZE] for i in range(0, weights.shape[1], HEAD_SIZE)]
    return functools.reduce(lambda a, b: a + b, parts)


def both_heads(ref, at):
    return jnp.concatenate([ref[at, :HEAD_SIZE], ref[at, HEAD_SIZE:]], axis=0)


def own_kernel(q_ref, k_ref, v_ref, sum_ref, weight_ref):
    for r in range(q_ref.shape[0] // 128):
        at = slice(r * 128, (r + 1) * 128)
        seen = (r + 1) * 128
        e = scores_of(both_heads(q_ref, at), k_ref[:seen])
        i = lax.broadcasted_iota(jnp.int32, e.shape, 0) % 128
        j = lax.broadcasted_iota(jnp.int32, e.shape, 1)
        e = jnp.where(j <= i + r * 128, e, 0.0)
        mixed = jnp.dot(e.astype(jnp.bfloat16), v_ref[:seen], preferred_element_type=jnp.float32)
        weight = lane_sums(e)
        for h in range(2):
            lanes = slice(h * HEAD_SIZE, (h + 1) * HEAD_SIZE)
            sum_ref[at, lanes] = mixed[h * 128 : (h + 1) * 128]
            weight_ref[at, lanes] = weight[h * 128 : (h + 1) * 128]


def behind_kernel(valid, q_ref, k1_ref, v1_ref, k2_ref, v2_ref, sum_ref, weight_ref, out_ref):
    has_one = valid[0].astype(jnp.float32)
    has_two = valid[1].astype(jnp.float32)
    rows = q_ref.shape[0]
    for r in range(rows // 128):
        at = slice(r * 128, (r + 1) * 128)
        q = both_heads(q_ref, at)
        one = scores_of(q, k1_ref[...])
        two = scores_of(q, k2_ref[r * 128 :])
        i = lax.broadcasted_iota(jnp.int32, two.shape, 0) % 128
        j = lax.broadcasted_iota(jnp.int32, two.shape, 1)
        two = jnp.where(j > i, two, 0.0)
        mixed = has_one * jnp.dot(
            one.astype(jnp.bfloat16), v1_ref[...], preferred_element_type=jnp.float32
        ) + has_two * jnp.dot(
            two.astype(jnp.bfloat16), v2_ref[r * 128 :], preferred_element_type=jnp.float32
        )
        weight = has_one * lane_sums(one) + has_two * lane_sums(two)
        for h in range(2):
            lanes = slice(h * HEAD_SIZE, (h + 1) * HEAD_SIZE)
            top = sum_ref[at, lanes] + mixed[h * 128 : (h + 1) * 128]
            low = jnp.sum(weight_ref[at, lanes] + weight[h * 128 : (h + 1) * 128], axis=-1, keepdims=True)
            out_ref[at, lanes] = (top / low).astype(jnp.bfloat16)


def attend_own(queries, keyed):
    rows, columns = queries.shape
    groups = columns // (2 * HEAD_SIZE)
    pair = pl.BlockSpec((rows, 2 * HEAD_SIZE), lambda g: (0, g))
    shape = jax.ShapeDtypeStruct((rows, columns), jnp.float32)
    return pl.pallas_call(
        own_kernel,
        grid=(groups,),
        in_specs=[
            pair,
            pl.BlockSpec((rows, HEAD_SIZE), lambda g: (0, g)),
            pl.BlockSpec((rows, HEAD_SIZE), lambda g: (0, groups + g)),
        ],
        out_specs=[pair, pair],
        out_shape=[shape, shape],
        compiler_params=pltpu.CompilerParams(vmem_limit_bytes=SMALL),
        cost_estimate=QUICK,
    )(queries, keyed, keyed)


def attend_behind(valid, queries, one, two, sums, weights):
    rows, columns = queries.shape
    groups = columns // (2 * HEAD_SIZE)
    pair = pl.BlockSpec((rows, 2 * HEAD_SIZE), lambda g, s: (0, g))
    keys = pl.BlockSpec((rows, HEAD_SIZE), lambda g, s: (0, g))
    values = pl.BlockSpec((rows, HEAD_SIZE), lambda g, s: (0, groups + g))
    return pl.pallas_call(
        behind_kernel,
        grid_spec=pltpu.PrefetchScalarGridSpec(
            num_scalar_prefetch=1,
            grid=(groups,),
            in_specs=[pair, keys, values, keys, values, pair, pair],
            out_specs=pair,
        ),
        out_shape=jax.ShapeDtypeStruct((rows, columns), jnp.bfloat16),
        compiler_params=pltpu.CompilerParams(vmem_limit_bytes=SMALL),
        cost_estimate=QUICK,
    )(valid, queries, one, one, two, two, sums, weights)


def half_kernel(half, weight_ref, context_ref, out_ref):
    out_ref[...] = lax.dot_general(
        weight_ref[...], context_ref[...], (((1,), (1,)), ((), ())), preferred_element_type=jnp.float32
    ).astype(out_ref.dtype)


def out_half(weight, context, half, dtype):
    rows, depth = context.shape
    columns = weight.shape[0] // 2
    steps = 4
    tile = columns // steps
    return pl.pallas_call(
        half_kernel,
        grid_spec=pltpu.PrefetchScalarGridSpec(
            num_scalar_prefetch=1,
            grid=(steps,),
            in_specs=[
                pl.BlockSpec((tile, depth), lambda i, s: (s[0] * steps + i, 0)),
                pl.BlockSpec((rows, depth), lambda i, s: (0, 0)),
            ],
            out_specs=pl.BlockSpec((tile, rows), lambda i, s: (i, 0)),
        ),
        out_shape=jax.ShapeDtypeStruct((columns, rows), dtype),
        compiler_params=pltpu.CompilerParams(vmem_limit_bytes=SMALL),
        cost_estimate=QUICK,
    )(half[None], weight, context)


def local(
    tokens, q_weight, key_matrix, value_matrix, o_weight, pre_gain, post_gain, q_gain, k_gain
):
    rows = tokens.shape[0]
    q_cols = q_weight.shape[1]
    yl, x, z, yh, c = (lax.axis_index(name) for name in ("yl", "x", "z", "yh", "c"))
    seq_index = (yl * 4 + x) * 4 + z
    whole = lax.all_gather(tokens.T, MP, axis=0)

    own = beside(q_weight, key_matrix, value_matrix)
    other = shift(own, "yl", 1)
    own_pieces = [own] + [shift(own, "x", step) for step in (1, 3, 2)]
    other_pieces = [other] + [shift(other, "z", step) for step in (1, 3, 2)]
    own_line = in_line(own_pieces, x)
    other_line = in_line(other_pieces, z)
    own_line, turned = lax.optimization_barrier((own_line, o_weight.T))
    own_ahead, own_behind = shift(own_line, "z", 1), shift(own_line, "z", 3)
    other_ahead, other_behind = shift(other_line, "x", 1), shift(other_line, "x", 3)
    near, far = norm_parts(whole, pre_gain, yl)

    y = yh * 2 + yl
    flat = lambda p: (p % 2) * 2 + p // 2
    one = lax.ppermute(turned, ("yl", "yh"), [(flat(a), flat(b)) for a, b in ((0, 1), (2, 0), (1, 3), (3, 2))])
    two = lax.ppermute(turned, ("yl", "yh"), [(flat(a), flat(b)) for a, b in ((1, 2), (2, 1))])
    positions = seq_index * rows + jnp.arange(rows, dtype=jnp.int32)
    half = HEAD_SIZE // 2
    freq = 10000.0 ** (-(jnp.arange(half, dtype=jnp.float32) * 2.0) / HEAD_SIZE)
    angle = positions.astype(jnp.float32)[:, None] * freq[None, :]
    cosine = jnp.cos(angle)
    sine = jnp.sin(angle)
    cosine = jnp.concatenate([cosine, cosine], axis=1)
    sine = jnp.concatenate([-sine, sine], axis=1)
    index = jnp.stack([z, (z + 3) % 4, (z + 1) % 4, x, (x + 3) % 4, (x + 1) % 4])

    outer = (y == 0) | (y == 3)
    pair = jnp.concatenate([jnp.where(outer, turned, one), jnp.where(outer, one, two)], axis=1)
    own_ahead, own_behind, other_ahead, other_behind, near, far, pair, cosine, sine, index = (
        lax.optimization_barrier(
            (own_ahead, own_behind, other_ahead, other_behind, near, far, pair, cosine, sine, index)
        )
    )

    own_far_kv = shift(cut(own_behind, 1), "z", 3)
    other_far_kv = shift(cut(other_behind, 1), "x", 3)
    own_far_q = shift(cut(own_ahead, 0), "z", 1)
    other_far_q = shift(cut(other_ahead, 0), "x", 1)
    out_all = lax.all_gather(pair, ("x", "z"), axis=0, tiled=True)
    parts = [own_line, own_ahead, own_behind], [other_line, other_ahead, other_behind]
    part_kv = early_product(1, index, near, far, *parts)
    part_kv, own_far_kv, other_far_kv = lax.optimization_barrier((part_kv, own_far_kv, other_far_kv))


    part_kv = part_kv + product(pick(near, z + 2), own_far_kv) + product(pick(far, x + 2), other_far_kv)
    keyed = finish_heads(2, part_kv, k_gain[None], cosine, sine)
    behind_one = from_behind(keyed, 1)
    behind_two = from_behind(keyed, 2)
    keyed, index = lax.optimization_barrier((keyed, index))
    part_q = early_product(0, index, near, far, *parts)
    part_q = part_q + product(pick(near, z + 2), own_far_q) + product(pick(far, x + 2), other_far_q)
    queries = finish_heads(4, part_q, q_gain[None], cosine, sine)
    sums, weights = attend_own(queries, keyed)
    valid = jnp.stack([seq_index >= 1, seq_index >= 2]).astype(jnp.int32)
    context = attend_behind(valid, queries, behind_one, behind_two, sums, weights)
    across = shift(context, "yh", 1)
    out_all, context = lax.optimization_barrier((out_all, context))
    both = jnp.concatenate([context, across], axis=1)

    half_of = functools.partial(out_half, out_all, both)
    received = shift(half_of(1 - c, jnp.bfloat16), "c", 1)
    kept, received = lax.optimization_barrier((half_of(c, jnp.float32), received))
    share = (kept + received.astype(jnp.float32)).T
    squares = jnp.sum(share * share, axis=1)
    squares = squares + shift(squares, "c", 1)
    total = squares + shift(squares, "yh", 1)
    scale_rows = lax.rsqrt(total / MODEL_WIDTH + epsilon)
    return (tokens.astype(jnp.float32) + share * scale_rows[:, None] * post_gain).astype(
        jnp.bfloat16
    )


def solution(mesh):
    fine = Mesh(np.asarray(mesh.devices).reshape(2, 4, 4, 2, 2), SEQ + MP)
    return jax.shard_map(
        local,
        mesh=fine,
        in_specs=(
            P(SEQ, MP),
            P(SEQ, MP),
            P(SEQ, MP),
            P(SEQ, MP),
            P(MP, SEQ),
            P(),
            P(MP),
            P(),
            P(),
        ),
        out_specs=P(SEQ, MP),
        check_vma=False,
    )
```

```python
import functools

import jax
import jax.numpy as jnp
import numpy as np
from jax import lax
from jax.experimental import pallas as pl
from jax.experimental.pallas import tpu as pltpu
from jax.sharding import Mesh, PartitionSpec as P

MODEL_WIDTH = 5376
HEAD_SIZE = 128
WINDOW_LENGTH = 1024
SHARD = MODEL_WIDTH // 32
VMEM = 40 << 20
SMALL = 16 << 20
LARGE = 58 << 20
QUICK = pl.CostEstimate(flops=0, bytes_accessed=0, transcendentals=0)

score_scale = 168.0 ** (-0.5)
epsilon = 1e-06
SEQ = ("yl", "x", "z")
MP = ("yh", "c")


def shift(value, axis, step):
    count = lax.axis_size(axis)
    return lax.ppermute(value, axis, [(i, (i + step) % count) for i in range(count)])


def from_behind(value, steps):
    count = 32
    return lax.ppermute(value, SEQ, [(source, source + steps) for source in range(count - steps)])


def later(values, done):
    return lax.optimization_barrier((values, done))[0]


def line_kernel(slots, *refs):
    for k, piece in enumerate(refs[:4]):

        @pl.when(pl.program_id(0) == k)
        def _():
            refs[4][0] = piece[...]


def in_line(pieces, at):
    depth, columns = pieces[0].shape
    line = pl.pallas_call(
        line_kernel,
        grid_spec=pltpu.PrefetchScalarGridSpec(
            num_scalar_prefetch=1,
            grid=(4,),
            in_specs=[pl.BlockSpec((depth, columns), lambda i, s: (0, 0))] * 4,
            out_specs=pl.BlockSpec((1, depth, columns), lambda i, s: (s[i], 0, 0)),
        ),
        out_shape=jax.ShapeDtypeStruct((4, depth, columns), jnp.bfloat16),
        compiler_params=pltpu.CompilerParams(vmem_limit_bytes=VMEM),
        cost_estimate=QUICK,
    )((at + jnp.array([0, 3, 1, 2], jnp.int32)) % 4, *pieces)
    return line.reshape(4 * depth, columns)


def beside_kernel(*refs):
    out_ref, start = refs[-1], 0
    for ref in refs[:-1]:
        out_ref[:, start : start + ref.shape[1]] = ref[...]
        start += ref.shape[1]


def beside(*values):
    rows, columns = values[0].shape[0], sum(value.shape[1] for value in values)
    return pl.pallas_call(
        beside_kernel,
        out_shape=jax.ShapeDtypeStruct((rows, columns), values[0].dtype),
        compiler_params=pltpu.CompilerParams(vmem_limit_bytes=LARGE),
        cost_estimate=QUICK,
    )(*values)


def cut_kernel(value_ref, out_ref):
    out_ref[...] = value_ref[...]


def cut(value, part):
    rows, columns = value.shape
    step = rows // 2
    return pl.pallas_call(
        cut_kernel,
        grid=(2,),
        in_specs=[pl.BlockSpec((step, columns // 2), lambda i: (i, part))],
        out_specs=pl.BlockSpec((step, columns // 2), lambda i: (i, 0)),
        out_shape=jax.ShapeDtypeStruct((rows, columns // 2), value.dtype),
        compiler_params=pltpu.CompilerParams(vmem_limit_bytes=VMEM),
        cost_estimate=QUICK,
    )(value)


def norm_kernel(side, own_ref, other_ref, near_gain, far_gain, near_ref, far_ref):
    own = own_ref[0].astype(jnp.float32)
    other = other_ref[0].astype(jnp.float32)
    total = jnp.sum(own * own, axis=(0, 1)) + jnp.sum(other * other, axis=(0, 1))
    scale = lax.rsqrt(total / MODEL_WIDTH + epsilon)[None, None]
    own = own * scale
    other = other * scale
    for i in range(4):
        starts = [(j // 2, ((j % 2) * 4 + i) * SHARD) for j in range(4)]
        part = jnp.concatenate([own[k, s : s + SHARD] for k, s in starts], axis=0)
        near_ref[i] = (part.T * near_gain[0, i]).astype(jnp.bfloat16)
        start = (i % 2) * 4 * SHARD
        part = other[i // 2, start : start + 4 * SHARD]
        far_ref[i] = (part.T * far_gain[0, i]).astype(jnp.bfloat16)


def norm_parts(pieces, gain, side):
    width, rows = pieces.shape[1:]
    step = 256
    pieces = pieces.reshape(2, 2, width, rows)
    far_gain = gain.reshape(2, 4, 4, SHARD)
    near_gain = jnp.swapaxes(far_gain, 1, 2).reshape(2, 4, 1, 4 * SHARD)
    far_gain = far_gain.reshape(2, 4, 1, 4 * SHARD)
    half = lambda flip: pl.BlockSpec((1, 2, width, step), lambda i, s: (s[flip], 0, 0, i))
    gains = lambda flip: pl.BlockSpec((1, 4, 1, 4 * SHARD), lambda i, s: (s[flip], 0, 0, 0))
    out = pl.BlockSpec((4, step, 4 * SHARD), lambda i, s: (0, i, 0))
    shape = jax.ShapeDtypeStruct((4, rows, 4 * SHARD), jnp.bfloat16)
    return pl.pallas_call(
        norm_kernel,
        grid_spec=pltpu.PrefetchScalarGridSpec(
            num_scalar_prefetch=1,
            grid=(rows // step,),
            in_specs=[half(0), half(1), gains(0), gains(1)],
            out_specs=[out, out],
        ),
        out_shape=[shape, shape],
        compiler_params=pltpu.CompilerParams(vmem_limit_bytes=LARGE),
        cost_estimate=QUICK,
    )(jnp.stack([side, 1 - side]), pieces, pieces, near_gain, far_gain)


def early_kernel(n_near, count, side, index, near_ref, far_ref, *refs):
    weights, (total, w_buf, t_buf, sems) = refs[:count], refs[count:]
    columns = total.shape[1]
    copies = []
    for k in range(count):
        source = near_ref if k < n_near else far_ref
        weight = weights[k].at[:, side * columns : (side + 1) * columns]
        copies.append(
            (
                pltpu.make_async_copy(source.at[index[k]], t_buf.at[k], sems.at[0, k]),
                pltpu.make_async_copy(weight, w_buf.at[k], sems.at[1, k]),
            )
        )
    for pair in copies:
        for copy in pair:
            copy.start()
    for k, pair in enumerate(copies):
        for copy in pair:
            copy.wait()
        part = jnp.dot(t_buf[k], w_buf[k], preferred_element_type=jnp.float32)
        total[...] = part if k == 0 else total[...] + part


def early_product(side, index, near, far, near_weights, far_weights):
    weights = near_weights + far_weights
    rows, depth, columns = near.shape[1], near.shape[2], weights[0].shape[1] // 2
    anywhere = pl.BlockSpec(memory_space=pl.ANY)
    count = len(weights)
    return pl.pallas_call(
        functools.partial(early_kernel, len(near_weights), count, side),
        grid_spec=pltpu.PrefetchScalarGridSpec(
            num_scalar_prefetch=1,
            grid=(1,),
            in_specs=[anywhere] * (2 + count),
            out_specs=pl.BlockSpec((rows, columns), lambda i, s: (0, 0)),
            scratch_shapes=[
                pltpu.VMEM((count, depth, columns), jnp.bfloat16),
                pltpu.VMEM((count, rows, depth), jnp.bfloat16),
                pltpu.SemaphoreType.DMA((2, count)),
            ],
        ),
        out_shape=jax.ShapeDtypeStruct((rows, columns), jnp.float32),
        compiler_params=pltpu.CompilerParams(vmem_limit_bytes=LARGE),
        cost_estimate=QUICK,
    )(index, near, far, *weights)


def pick(parts, at):
    return lax.dynamic_index_in_dim(parts, at % 4, 0, keepdims=False)


def product(left, right):
    return jnp.dot(left, right, preferred_element_type=jnp.float32)


def turned_heads(raw, gain, cosine, sine):
    normal = raw * lax.rsqrt(jnp.mean(raw * raw, axis=-1, keepdims=True) + epsilon) * gain
    return normal * cosine + pltpu.roll(normal, HEAD_SIZE // 2, 1) * sine


def heads_kernel(heads, raw_ref, gain, cosine, sine, out_ref):
    for h in range(raw_ref.shape[1] // HEAD_SIZE):
        lanes = slice(h * HEAD_SIZE, (h + 1) * HEAD_SIZE)
        raw = raw_ref[:, lanes]
        if h < heads:
            raw = turned_heads(raw, gain[...], cosine[...], sine[...])
        out_ref[:, lanes] = raw.astype(jnp.bfloat16)


def finish_heads(heads, raw, gain, cosine, sine):
    rows, columns = raw.shape
    step = 256
    block = pl.BlockSpec((step, columns), lambda i: (i, 0))
    table = pl.BlockSpec((step, HEAD_SIZE), lambda i: (i, 0))
    return pl.pallas_call(
        functools.partial(heads_kernel, heads),
        grid=(rows // step,),
        in_specs=[block, pl.BlockSpec((1, HEAD_SIZE), lambda i: (0, 0)), table, table],
        out_specs=block,
        out_shape=jax.ShapeDtypeStruct((rows, columns), jnp.bfloat16),
        compiler_params=pltpu.CompilerParams(vmem_limit_bytes=SMALL),
        cost_estimate=QUICK,
    )(raw, gain, cosine, sine)


def scores_of(queries, keys):
    score = lax.dot_general(
        queries, keys, (((1,), (1,)), ((), ())), preferred_element_type=jnp.float32
    )
    return jnp.exp(score * score_scale)


def lane_sums(weights):
    parts = [weights[:, i : i + HEAD_SIZE] for i in range(0, weights.shape[1], HEAD_SIZE)]
    return functools.reduce(lambda a, b: a + b, parts)


def both_heads(ref, at):
    return jnp.concatenate([ref[at, :HEAD_SIZE], ref[at, HEAD_SIZE:]], axis=0)


def own_kernel(q_ref, k_ref, v_ref, sum_ref, weight_ref):
    for r in range(q_ref.shape[0] // 128):
        at = slice(r * 128, (r + 1) * 128)
        seen = (r + 1) * 128
        e = scores_of(both_heads(q_ref, at), k_ref[:seen])
        i = lax.broadcasted_iota(jnp.int32, e.shape, 0) % 128
        j = lax.broadcasted_iota(jnp.int32, e.shape, 1)
        e = jnp.where(j <= i + r * 128, e, 0.0)
        mixed = jnp.dot(e.astype(jnp.bfloat16), v_ref[:seen], preferred_element_type=jnp.float32)
        weight = lane_sums(e)
        for h in range(2):
            lanes = slice(h * HEAD_SIZE, (h + 1) * HEAD_SIZE)
            sum_ref[at, lanes] = mixed[h * 128 : (h + 1) * 128]
            weight_ref[at, lanes] = weight[h * 128 : (h + 1) * 128]


def behind_kernel(valid, q_ref, k1_ref, v1_ref, k2_ref, v2_ref, sum_ref, weight_ref, out_ref):
    has_one = valid[0].astype(jnp.float32)
    has_two = valid[1].astype(jnp.float32)
    rows = q_ref.shape[0]
    for r in range(rows // 128):
        at = slice(r * 128, (r + 1) * 128)
        q = both_heads(q_ref, at)
        one = scores_of(q, k1_ref[...])
        two = scores_of(q, k2_ref[r * 128 :])
        i = lax.broadcasted_iota(jnp.int32, two.shape, 0) % 128
        j = lax.broadcasted_iota(jnp.int32, two.shape, 1)
        two = jnp.where(j > i, two, 0.0)
        mixed = has_one * jnp.dot(
            one.astype(jnp.bfloat16), v1_ref[...], preferred_element_type=jnp.float32
        ) + has_two * jnp.dot(
            two.astype(jnp.bfloat16), v2_ref[r * 128 :], preferred_element_type=jnp.float32
        )
        weight = has_one * lane_sums(one) + has_two * lane_sums(two)
        for h in range(2):
            lanes = slice(h * HEAD_SIZE, (h + 1) * HEAD_SIZE)
            top = sum_ref[at, lanes] + mixed[h * 128 : (h + 1) * 128]
            low = jnp.sum(weight_ref[at, lanes] + weight[h * 128 : (h + 1) * 128], axis=-1, keepdims=True)
            out_ref[at, lanes] = (top / low).astype(jnp.bfloat16)


def attend_own(queries, keyed):
    rows, columns = queries.shape
    groups = columns // (2 * HEAD_SIZE)
    pair = pl.BlockSpec((rows, 2 * HEAD_SIZE), lambda g: (0, g))
    shape = jax.ShapeDtypeStruct((rows, columns), jnp.float32)
    return pl.pallas_call(
        own_kernel,
        grid=(groups,),
        in_specs=[
            pair,
            pl.BlockSpec((rows, HEAD_SIZE), lambda g: (0, g)),
            pl.BlockSpec((rows, HEAD_SIZE), lambda g: (0, groups + g)),
        ],
        out_specs=[pair, pair],
        out_shape=[shape, shape],
        compiler_params=pltpu.CompilerParams(vmem_limit_bytes=SMALL),
        cost_estimate=QUICK,
    )(queries, keyed, keyed)


def attend_behind(valid, queries, one, two, sums, weights):
    rows, columns = queries.shape
    groups = columns // (2 * HEAD_SIZE)
    pair = pl.BlockSpec((rows, 2 * HEAD_SIZE), lambda g, s: (0, g))
    keys = pl.BlockSpec((rows, HEAD_SIZE), lambda g, s: (0, g))
    values = pl.BlockSpec((rows, HEAD_SIZE), lambda g, s: (0, groups + g))
    return pl.pallas_call(
        behind_kernel,
        grid_spec=pltpu.PrefetchScalarGridSpec(
            num_scalar_prefetch=1,
            grid=(groups,),
            in_specs=[pair, keys, values, keys, values, pair, pair],
            out_specs=pair,
        ),
        out_shape=jax.ShapeDtypeStruct((rows, columns), jnp.bfloat16),
        compiler_params=pltpu.CompilerParams(vmem_limit_bytes=SMALL),
        cost_estimate=QUICK,
    )(valid, queries, one, one, two, two, sums, weights)


def half_kernel(half, weight_ref, context_ref, out_ref):
    out_ref[...] = lax.dot_general(
        weight_ref[...], context_ref[...], (((1,), (1,)), ((), ())), preferred_element_type=jnp.float32
    ).astype(out_ref.dtype)


def out_half(weight, context, half, dtype):
    rows, depth = context.shape
    columns = weight.shape[0] // 2
    steps = 2
    tile = columns // steps
    return pl.pallas_call(
        half_kernel,
        grid_spec=pltpu.PrefetchScalarGridSpec(
            num_scalar_prefetch=1,
            grid=(steps,),
            in_specs=[
                pl.BlockSpec((tile, depth), lambda i, s: (s[0] * steps + i, 0)),
                pl.BlockSpec((rows, depth), lambda i, s: (0, 0)),
            ],
            out_specs=pl.BlockSpec((tile, rows), lambda i, s: (i, 0)),
        ),
        out_shape=jax.ShapeDtypeStruct((columns, rows), dtype),
        compiler_params=pltpu.CompilerParams(vmem_limit_bytes=SMALL),
        cost_estimate=QUICK,
    )(half[None], weight, context)


def local(
    tokens, q_weight, key_matrix, value_matrix, o_weight, pre_gain, post_gain, q_gain, k_gain
):
    rows = tokens.shape[0]
    q_cols = q_weight.shape[1]
    yl, x, z, yh, c = (lax.axis_index(name) for name in ("yl", "x", "z", "yh", "c"))
    seq_index = (yl * 4 + x) * 4 + z
    whole = lax.all_gather(tokens.T, MP, axis=0)

    own = beside(q_weight, key_matrix, value_matrix)
    other = shift(own, "yl", 1)
    own_pieces = [own] + [shift(own, "x", step) for step in (1, 3, 2)]
    other_pieces = [other] + [shift(other, "z", step) for step in (1, 3, 2)]
    own_line = in_line(own_pieces, x)
    other_line = in_line(other_pieces, z)
    own_line, turned = lax.optimization_barrier((own_line, o_weight.T))
    own_ahead, own_behind = shift(own_line, "z", 1), shift(own_line, "z", 3)
    other_ahead, other_behind = shift(other_line, "x", 1), shift(other_line, "x", 3)
    near, far = norm_parts(whole, pre_gain, yl)

    y = yh * 2 + yl
    flat = lambda p: (p % 2) * 2 + p // 2
    one = lax.ppermute(turned, ("yl", "yh"), [(flat(a), flat(b)) for a, b in ((0, 1), (2, 0), (1, 3), (3, 2))])
    two = lax.ppermute(turned, ("yl", "yh"), [(flat(a), flat(b)) for a, b in ((1, 2), (2, 1))])
    positions = seq_index * rows + jnp.arange(rows, dtype=jnp.int32)
    half = HEAD_SIZE // 2
    freq = 10000.0 ** (-(jnp.arange(half, dtype=jnp.float32) * 2.0) / HEAD_SIZE)
    angle = positions.astype(jnp.float32)[:, None] * freq[None, :]
    cosine = jnp.cos(angle)
    sine = jnp.sin(angle)
    cosine = jnp.concatenate([cosine, cosine], axis=1)
    sine = jnp.concatenate([-sine, sine], axis=1)
    index = jnp.stack([z, (z + 3) % 4, (z + 1) % 4, x, (x + 3) % 4, (x + 1) % 4])

    outer = (y == 0) | (y == 3)
    pair = jnp.concatenate([jnp.where(outer, turned, one), jnp.where(outer, one, two)], axis=1)
    own_ahead, own_behind, other_ahead, other_behind, near, far, pair, cosine, sine, index = (
        lax.optimization_barrier(
            (own_ahead, own_behind, other_ahead, other_behind, near, far, pair, cosine, sine, index)
        )
    )

    own_far_kv = shift(cut(own_behind, 1), "z", 3)
    other_far_kv = shift(cut(other_behind, 1), "x", 3)
    own_far_q = shift(cut(own_ahead, 0), "z", 1)
    other_far_q = shift(cut(other_ahead, 0), "x", 1)
    out_all = lax.all_gather(pair, ("x", "z"), axis=0, tiled=True)
    parts = [own_line, own_ahead, own_behind], [other_line, other_ahead, other_behind]
    part_kv = early_product(1, index, near, far, *parts)
    part_kv, own_far_kv, other_far_kv = lax.optimization_barrier((part_kv, own_far_kv, other_far_kv))


    part_kv = part_kv + product(pick(near, z + 2), own_far_kv) + product(pick(far, x + 2), other_far_kv)
    keyed = finish_heads(2, part_kv, k_gain[None], cosine, sine)
    behind_one = from_behind(keyed, 1)
    behind_two = from_behind(keyed, 2)
    keyed, index = lax.optimization_barrier((keyed, index))
    part_q = early_product(0, index, near, far, *parts)
    part_q = part_q + product(pick(near, z + 2), own_far_q) + product(pick(far, x + 2), other_far_q)
    queries = finish_heads(4, part_q, q_gain[None], cosine, sine)
    sums, weights = attend_own(queries, keyed)
    valid = jnp.stack([seq_index >= 1, seq_index >= 2]).astype(jnp.int32)
    context = attend_behind(valid, queries, behind_one, behind_two, sums, weights)
    across = shift(context, "yh", 1)
    out_all, context = lax.optimization_barrier((out_all, context))
    both = jnp.concatenate([context, across], axis=1)

    half_of = functools.partial(out_half, out_all, both)
    received = shift(half_of(1 - c, jnp.bfloat16), "c", 1)
    kept, received = lax.optimization_barrier((half_of(c, jnp.float32), received))
    share = (kept + received.astype(jnp.float32)).T
    squares = jnp.sum(share * share, axis=1)
    squares = squares + shift(squares, "c", 1)
    total = squares + shift(squares, "yh", 1)
    scale_rows = lax.rsqrt(total / MODEL_WIDTH + epsilon)
    return (tokens.astype(jnp.float32) + share * scale_rows[:, None] * post_gain).astype(
        jnp.bfloat16
    )


def solution(mesh):
    fine = Mesh(np.asarray(mesh.devices).reshape(2, 4, 4, 2, 2), SEQ + MP)
    return jax.shard_map(
        local,
        mesh=fine,
        in_specs=(
            P(SEQ, MP),
            P(SEQ, MP),
            P(SEQ, MP),
            P(SEQ, MP),
            P(MP, SEQ),
            P(),
            P(MP),
            P(),
            P(),
        ),
        out_specs=P(SEQ, MP),
        check_vma=False,
    )
```
